256 devices in a mesh: tensor: 4 (over y_lo, core), context: 64 (over y_hi, x, z).
Axes of the slice: x: 4, y: 4 (y_hi: 2, y_lo: 2; y = y_hi * 2 + y_lo), z: 8, core: 2. Of those that a mesh axis runs over, the one named last changes fastest.
Arguments:
- hidden_in: bfloat16 [64, 128, 4096], P('context'), may hold values from -12 to 12
- value_first: bfloat16 [64, 128, 512], P('context', None, 'tensor'), may hold values from -6 to 6
- w_query: bfloat16 [4096, 2048], P(None, 'tensor'), may hold values from -0.09375 to 0.09375
- w_key: bfloat16 [4096, 512], P(None, 'tensor'), may hold values from -0.09375 to 0.09375
- w_value: bfloat16 [4096, 512], P(None, 'tensor'), may hold values from -0.09375 to 0.09375
- w_out: bfloat16 [2048, 4096], P('tensor'), may hold values from -0.125 to 0.125
- value_mix: float32 [2, 4], P(None, 'tensor'), may hold values from 0.2 to 1
- grad_out: bfloat16 [64, 128, 4096], P('context', 'tensor'), may hold values from -3 to 3
Outputs:
- attn_out: bfloat16 [64, 128, 4096], P('context', 'tensor')
- grad_in: bfloat16 [64, 128, 4096], P('context', 'tensor')
- grad_value_first: bfloat16 [64, 128, 512], P('context', None, 'tensor')
- grad_w_key: float32 [4096, 512], P('context', 'tensor')
- grad_w_value: float32 [4096, 512], P('context', 'tensor')
The draws below stay inside these ranges and needn't reach their ends.
All inputs are finite; a program needn't handle non-finite values.
Results may differ from the reference program's by a relative error of at most 0.03.
The reference program's roundings to bfloat16 on the way count: a program that leaves them out, or rounds other values in their place, can miss the bound.
Values may be sent and summed in bfloat16 or wider, within the bound.
A program may use at most 128 MiB of HBM per device.

```python
import jax
import jax.numpy as jnp
from jax import lax

D = 4096
HEADS = 16
KVH = 4
HD = 128
TOK_DEV = 128
GROUP = 4
QD = 2048
KVD = 512
BLOCKS = 64
TOKENS = 8192


def draw_hidden_in(key, part):
    key = jax.random.fold_in(key, 11)
    base_key = jax.random.fold_in(key, 0)
    full_shape = (BLOCKS, TOK_DEV, D)
    entries = jax.random.normal(base_key, full_shape, jnp.float32)
    return jnp.clip(entries, -6.0, 6.0).astype(jnp.bfloat16)


def block_scale(stream_key, extent, shards, low, top_value):
    loudness = 1.0
    for axis_at, parts in shards:
        draws = jax.random.uniform(jax.random.fold_in(jax.random.fold_in(stream_key, 6), axis_at), (parts,), jnp.float32, low / len(shards), top_value / len(shards))
        loudness = loudness * jnp.repeat(jnp.exp(draws), extent[axis_at] // parts).reshape((-1,) + (1,) * (len(extent) - 1 - axis_at))
    return loudness


def normal_values(stream_key, shape, deviation, limit, cuts=(), kind=jnp.bfloat16):
    loudness = block_scale(stream_key, shape, cuts, -0.22, 0.18) if cuts else 1.0
    array = jax.random.normal(stream_key, shape, jnp.float32) * deviation * loudness
    return jnp.minimum(jnp.maximum(array, -limit), limit).astype(kind)


def setup_inputs(seed: int = 0) -> dict:
    key_of = jax.random.split(jax.random.key(seed), 9)
    return {
        "hidden_in": draw_hidden_in(jax.random.fold_in(key_of[8], 71), 0),
        "value_first": normal_values(key_of[1], (BLOCKS, TOK_DEV, KVD), 1.0, 6.0, ((0, 64), (2, 4))),
        "w_query": normal_values(key_of[2], (D, QD), D ** -0.5, 0.09375, ((1, 4),)),
        "w_key": normal_values(key_of[3], (D, KVD), D ** -0.5, 0.09375, ((1, 4),)),
        "w_value": normal_values(key_of[4], (D, KVD), D ** -0.5, 0.09375, ((1, 4),)),
        "w_out": normal_values(key_of[5], (QD, D), QD ** -0.5, 0.125, ((0, 4),)),
        "value_mix": jnp.clip(0.2 + 0.8 * jax.random.uniform(key_of[6], (2, KVH), jnp.float32) ** block_scale(key_of[6], (2, KVH), ((1, 4),), -0.2, 0.2), 0.2, 1.0),
        "grad_out": normal_values(key_of[7], (BLOCKS, TOK_DEV, D), 0.5, 3.0, ((0, 64), (1, 4))),
    }


THETA = 500000.0
NEGATIVE = -1.0e30


def rope_tables(positions, head_width):
    half_width = head_width // 2
    exponent = jnp.arange(half_width, dtype=jnp.float32) * (2.0 / head_width)
    frequency = jnp.power(jnp.float32(THETA), -exponent)
    angles = positions.astype(jnp.float32)[:, None] * frequency[None, :]
    return jnp.cos(angles), jnp.sin(angles)


def rotate(field, cosine_table, sine_table):
    half_width = field.shape[-1] // 2
    first_half = field[..., :half_width]
    second_half = field[..., half_width:]
    cosine_part = cosine_table[:, None, :]
    sine_part = sine_table[:, None, :]
    return jnp.concatenate([first_half * cosine_part - second_half * sine_part, second_half * cosine_part + first_half * sine_part], axis=-1)


def reference(hidden_in, value_first, w_query, w_key, w_value, w_out, value_mix, grad_out):
    seq_len = TOKENS
    score_scale = HD ** -0.5
    inputs = hidden_in.reshape(seq_len, D)
    firsts = value_first.reshape(seq_len, KVH, HD)
    grads = grad_out.reshape(seq_len, D)
    positions = jnp.arange(seq_len, dtype=jnp.int32)
    causal = positions[:, None] >= positions[None, :]
    cosine_table, sine_table = rope_tables(positions, HD)
    query_raw = jnp.dot(inputs, w_query, preferred_element_type=jnp.float32).reshape(seq_len, HEADS, HD)
    queries = rotate(query_raw, cosine_table, sine_table).astype(jnp.bfloat16)
    key_raw = jnp.dot(inputs, w_key, preferred_element_type=jnp.float32).reshape(seq_len, KVH, HD)
    key_rows = rotate(key_raw, cosine_table, sine_table).astype(jnp.bfloat16)
    value_proj = jnp.dot(inputs, w_value, preferred_element_type=jnp.float32).reshape(seq_len, KVH, HD)
    mixed_values = (value_mix[0][None, :, None] * value_proj + value_mix[1][None, :, None] * firsts.astype(jnp.float32)).astype(jnp.bfloat16)
    query_heads = queries.transpose(1, 0, 2)
    key_heads = jnp.repeat(key_rows.transpose(1, 0, 2), GROUP, axis=0)
    value_heads = jnp.repeat(mixed_values.transpose(1, 0, 2), GROUP, axis=0)

    def head_forward(operands):
        query_head, key_head, value_head = operands
        scores = jnp.dot(query_head, key_head.T, preferred_element_type=jnp.float32) * score_scale
        masked = jnp.where(causal, scores, NEGATIVE)
        row_max = jnp.max(masked, axis=1, keepdims=True)
        totals = jnp.sum(jnp.where(causal, jnp.exp(masked - row_max), 0.0), axis=1, keepdims=True)
        log_total = row_max + jnp.log(totals)
        weights = jnp.where(causal, jnp.exp(masked - log_total), 0.0).astype(jnp.bfloat16)
        output = jnp.dot(weights, value_head, preferred_element_type=jnp.float32).astype(jnp.bfloat16)
        return output, log_total[:, 0]

    out_heads, log_totals = lax.map(head_forward, (query_heads, key_heads, value_heads))
    outputs = out_heads.transpose(1, 0, 2).reshape(seq_len, QD)
    attn_out = jnp.dot(outputs, w_out, preferred_element_type=jnp.float32).astype(jnp.bfloat16)
    dout = jnp.dot(grads, w_out.T, preferred_element_type=jnp.float32).astype(jnp.bfloat16)
    dout_heads = dout.reshape(seq_len, HEADS, HD).transpose(1, 0, 2)

    def head_backward(operands):
        query_head, key_head, value_head, output_head, dout_head, log_total = operands
        scores = jnp.dot(query_head, key_head.T, preferred_element_type=jnp.float32) * score_scale
        masked = jnp.where(causal, scores, NEGATIVE)
        probabilities = jnp.where(causal, jnp.exp(masked - log_total[:, None]), 0.0)
        row_delta = jnp.sum(dout_head.astype(jnp.float32) * output_head.astype(jnp.float32), axis=1)
        prob_grads = jnp.dot(dout_head, value_head.T, preferred_element_type=jnp.float32)
        score_grads = (probabilities * (prob_grads - row_delta[:, None])).astype(jnp.bfloat16)
        query_grad = jnp.dot(score_grads, key_head, preferred_element_type=jnp.float32) * score_scale
        key_grad = jnp.dot(score_grads.T, query_head, preferred_element_type=jnp.float32) * score_scale
        value_grad = jnp.dot(probabilities.astype(jnp.bfloat16).T, dout_head, preferred_element_type=jnp.float32)
        return query_grad, key_grad, value_grad

    query_grads, key_grads, value_grads = lax.map(head_backward, (query_heads, key_heads, value_heads, out_heads, dout_heads, log_totals))
    key_sum = key_grads.reshape(KVH, GROUP, seq_len, HD).sum(axis=1).transpose(1, 0, 2)
    value_sum = value_grads.reshape(KVH, GROUP, seq_len, HD).sum(axis=1).transpose(1, 0, 2)
    query_pre = rotate(query_grads.transpose(1, 0, 2), cosine_table, -sine_table).astype(jnp.bfloat16).reshape(seq_len, QD)
    key_pre = rotate(key_sum, cosine_table, -sine_table).astype(jnp.bfloat16).reshape(seq_len, KVD)
    value_pre = (value_mix[0][None, :, None] * value_sum).astype(jnp.bfloat16).reshape(seq_len, KVD)
    first_grad = (value_mix[1][None, :, None] * value_sum).astype(jnp.bfloat16).reshape(seq_len, KVD)
    input_sum = jnp.dot(query_pre, w_query.T, preferred_element_type=jnp.float32)
    input_sum = input_sum + jnp.dot(key_pre, w_key.T, preferred_element_type=jnp.float32)
    input_sum = input_sum + jnp.dot(value_pre, w_value.T, preferred_element_type=jnp.float32)
    grad_in = input_sum.astype(jnp.bfloat16)
    grad_w_key = jnp.dot(inputs.T, key_pre, preferred_element_type=jnp.float32)
    grad_w_value = jnp.dot(inputs.T, value_pre, preferred_element_type=jnp.float32)
    return (attn_out.reshape(BLOCKS, TOK_DEV, D), grad_in.reshape(BLOCKS, TOK_DEV, D), first_grad.reshape(BLOCKS, TOK_DEV, KVD), grad_w_key, grad_w_value)
```

```python
import jax
import jax.numpy as jnp
from jax import lax
from jax.experimental import pallas as pl
from jax.experimental.pallas import tpu as pltpu
from jax.sharding import PartitionSpec as P

HD = 128
THETA = 500000.0
LOG2E = 1.4426950408889634
NEGATIVE = -1e30
NY, NX, NZ = 2, 4, 8
TILE = 512
F32, BF16 = jnp.float32, jnp.bfloat16


def position():
    rank = lax.axis_index("context")
    return rank // (NX * NZ), (rank // NZ) % NX, rank % NZ


def rank_of(y, x, z):
    return (y * NX + x) * NZ + z


def turn(value, step, count):
    return lax.rem(value + (step + count), count)


def remote(source, target, send_sem, recv_sem, rank):
    return pltpu.make_async_remote_copy(
        src_ref=source,
        dst_ref=target,
        send_sem=send_sem,
        recv_sem=recv_sem,
        device_id={"context": rank},
        device_id_type=pl.DeviceIdType.MESH,
    )


def greet(y, x, z):
    barrier = pltpu.get_barrier_semaphore()
    ranks = [rank_of(1 - y, x, z), rank_of(y, x, turn(z, 1, NZ)), rank_of(y, x, turn(z, -1, NZ))]
    ranks += [rank_of(y, turn(x, step, NX), z) for step in (1, 2, 3)]
    for rank in ranks:
        pl.semaphore_signal(
            barrier, inc=1, device_id={"context": rank}, device_id_type=pl.DeviceIdType.MESH
        )
    pl.semaphore_wait(barrier, len(ranks))


CHAINS = ((1, 0, "long"), (1, 1, "short"), (-1, 1, "long"), (-1, 0, "short"))


def gather_kernel(
    k_in, v_in, k_all, v_all, y_send, y_recv, kx_send, kx_recv, vz_send, vz_recv, kz_send, kz_recv,
    vx_send, vx_recv,
):
    y, x, z = position()
    k_all[y, x, z] = k_in[...]
    v_all[y, x, z] = v_in[...]
    greet(y, x, z)
    started = []

    def go(copy):
        copy.start()
        started.append(copy)
        return copy

    partner = rank_of(1 - y, x, z)
    k_pair = go(remote(k_in, k_all.at[y, x, z], y_send.at[0], y_recv.at[0], partner))
    v_pair = go(remote(v_in, v_all.at[y, x, z], y_send.at[1], y_recv.at[1], partner))

    def vz_hop(chain, hop):
        way, half, _ = CHAINS[chain]
        part = v_all.at[half, x, turn(z, -way * hop, NZ)]
        return go(
            remote(
                part, part, vz_send.at[chain, hop], vz_recv.at[chain, hop],
                rank_of(y, x, turn(z, way, NZ)),
            )
        )

    def kz_hop(chain, hop):
        way, half, _ = CHAINS[chain]
        part = k_all.at[half, :, turn(z, -way * hop, NZ)]
        return go(
            remote(
                part, part, kz_send.at[chain, hop], kz_recv.at[chain, hop],
                rank_of(y, x, turn(z, way, NZ)),
            )
        )

    def vx_hop(chain, hop):
        way, half, _ = CHAINS[chain]
        part = v_all.at[half, turn(x, -way * hop, NX)]
        return go(
            remote(
                part, part, vx_send.at[chain, hop], vx_recv.at[chain, hop],
                rank_of(y, turn(x, way, NX), z),
            )
        )

    k_pair.wait_recv()
    kx = []
    for step in (1, 2, 3):
        part = k_all.at[:, x, z]
        kx.append(
            go(
                remote(
                    part, part, kx_send.at[step - 1], kx_recv.at[step - 1],
                    rank_of(y, turn(x, step, NX), z),
                )
            )
        )
    v_pair.wait_recv()
    all_chains, long_chains = (0, 1, 2, 3), (0, 2)
    vz = {chain: vz_hop(chain, 0) for chain in all_chains}
    for copy in kx:
        copy.wait_recv()
    kz = {chain: kz_hop(chain, 0) for chain in all_chains}

    def advance(flight, hop_of, hop, chains):
        for chain in chains:
            flight[chain].wait_recv()
            flight[chain] = hop_of(chain, hop)

    advance(vz, vz_hop, 1, all_chains)
    advance(vz, vz_hop, 2, all_chains)
    advance(kz, kz_hop, 1, all_chains)
    advance(vz, vz_hop, 3, long_chains)
    for chain in all_chains:
        vz[chain].wait_recv()
    vx = {chain: vx_hop(chain, 0) for chain in all_chains}
    advance(kz, kz_hop, 2, all_chains)
    advance(kz, kz_hop, 3, long_chains)
    for chain in long_chains:
        vx[chain].wait_recv()
        vx[chain] = vx_hop(chain, 1)
    for chain in all_chains:
        kz[chain].wait_recv()
        vx[chain].wait_recv()
    for copy in started:
        copy.wait_send()


def gather_blocks(key_rows, value_rows):
    rows = key_rows.shape[0]
    whole = jax.ShapeDtypeStruct((NY, NX, NZ, rows, HD), BF16)
    vmem = pl.BlockSpec(memory_space=pltpu.VMEM)
    dma = pltpu.SemaphoreType.DMA
    return pl.pallas_call(
        gather_kernel,
        out_shape=(whole, whole),
        in_specs=[vmem] * 2,
        out_specs=(vmem, vmem),
        scratch_shapes=[
            dma((2,)), dma((2,)), dma((3,)), dma((3,)), dma((4, 4)), dma((4, 4)), dma((4, 4)),
            dma((4, 4)), dma((4, 2)), dma((4, 2)),
        ],
        compiler_params=pltpu.CompilerParams(
            collective_id=1, has_side_effects=True, vmem_limit_bytes=24 * 2**20
        ),
        name="gather_blocks",
    )(key_rows, value_rows)


def add_into(target, term):
    target[...] = (target[...].astype(F32) + term[...].astype(F32)).astype(BF16)


def scatter_kernel(
    a_in, b_in, a_out, b_out, az_buf, bx_buf, bz_buf, a_sum, b_sum, ax_buf, a_low, b_low, y_buf,
    az_send, az_recv, bx_send, bx_recv, bz_send, bz_recv, ax_send, ax_recv, y_send, y_recv,
):
    y, x, z = position()
    greet(y, x, z)
    started = []

    def go(copy):
        copy.start()
        started.append(copy)
        return copy

    def az_hop(chain, hop, hops):
        way, half, _ = CHAINS[chain]
        far = turn(z, way * (hops - hop), NZ)
        own = a_in.at[half, :, far]
        source = own
        if hop:
            source = az_buf.at[chain, hop - 1]
            add_into(source, own)
        return go(
            remote(
                source, az_buf.at[chain, hop], az_send.at[chain, hop], az_recv.at[chain, hop],
                rank_of(y, x, turn(z, way, NZ)),
            )
        )

    def bx_hop(chain, hop, hops):
        way, half, _ = CHAINS[chain]
        far = turn(x, way * (hops - hop), NX)
        own = b_in.at[half, far]
        source = own
        if hop:
            source = bx_buf.at[chain, hop - 1]
            add_into(source, own)
        return go(
            remote(
                source, bx_buf.at[chain, hop], bx_send.at[chain, hop], bx_recv.at[chain, hop],
                rank_of(y, turn(x, way, NX), z),
            )
        )

    def bz_hop(chain, hop, hops):
        way, half, _ = CHAINS[chain]
        far = turn(z, way * (hops - hop), NZ)
        own = b_sum.at[half, far]
        source = own
        if hop:
            source = bz_buf.at[chain, hop - 1]
            add_into(source, own)
        return go(
            remote(
                source, bz_buf.at[chain, hop], bz_send.at[chain, hop], bz_recv.at[chain, hop],
                rank_of(y, x, turn(z, way, NZ)),
            )
        )

    z_hops = {0: 4, 1: 3, 2: 4, 3: 3}
    x_hops = {0: 2, 1: 1, 2: 2, 3: 1}
    order = (0, 2, 1, 3)
    az = {chain: az_hop(chain, 0, z_hops[chain]) for chain in order}
    bx = {chain: bx_hop(chain, 0, x_hops[chain]) for chain in order}

    def advance(flight, hop_of, hop, hops):
        for chain in order:
            if hop < hops[chain]:
                flight[chain].wait_recv()
                flight[chain] = hop_of(chain, hop, hops[chain])

    advance(az, az_hop, 1, z_hops)
    advance(bx, bx_hop, 1, x_hops)
    advance(az, az_hop, 2, z_hops)
    for chain in order:
        bx[chain].wait_recv()
    for half in range(NY):
        right, left = (0, 3) if half == 0 else (1, 2)
        b_sum[half] = (
            b_in[half, x].astype(F32)
            + bx_buf[right, x_hops[right] - 1].astype(F32)
            + bx_buf[left, x_hops[left] - 1].astype(F32)
        ).astype(BF16)
    bz = {chain: bz_hop(chain, 0, z_hops[chain]) for chain in order}
    advance(az, az_hop, 3, z_hops)
    advance(bz, bz_hop, 1, z_hops)
    for chain in order:
        az[chain].wait_recv()
    for half in range(NY):
        right, left = (0, 3) if half == 0 else (1, 2)
        a_sum[:, half] = (
            a_in[half, :, z].astype(F32)
            + az_buf[right, z_hops[right] - 1].astype(F32)
            + az_buf[left, z_hops[left] - 1].astype(F32)
        ).astype(BF16)
    ax = []
    for step in (1, 2, 3):
        other = turn(x, step, NX)
        ax.append(
            go(
                remote(
                    a_sum.at[other], ax_buf.at[step - 1], ax_send.at[step - 1],
                    ax_recv.at[step - 1], rank_of(y, other, z),
                )
            )
        )
    advance(bz, bz_hop, 2, z_hops)
    for copy in ax:
        copy.wait_recv()
    a_total = a_sum[x].astype(F32)
    for step in range(3):
        a_total = a_total + ax_buf[step].astype(F32)
    a_low[...] = a_total.astype(BF16)
    partner = rank_of(1 - y, x, z)
    a_pair = go(remote(a_low.at[1 - y], y_buf.at[0], y_send.at[0], y_recv.at[0], partner))
    advance(bz, bz_hop, 3, z_hops)
    for chain in order:
        bz[chain].wait_recv()
    for half in range(NY):
        right, left = (0, 3) if half == 0 else (1, 2)
        b_low[half] = (
            b_sum[half, z].astype(F32)
            + bz_buf[right, z_hops[right] - 1].astype(F32)
            + bz_buf[left, z_hops[left] - 1].astype(F32)
        ).astype(BF16)
    b_pair = go(remote(b_low.at[1 - y], y_buf.at[1], y_send.at[1], y_recv.at[1], partner))
    a_pair.wait_recv()
    a_out[...] = a_low[y].astype(F32) + y_buf[0].astype(F32)
    b_pair.wait_recv()
    b_out[...] = b_low[y].astype(F32) + y_buf[1].astype(F32)
    for copy in started:
        copy.wait_send()


def scatter_blocks(a_parts, b_parts, identity, name):
    rows = a_parts.shape[-2]
    one = jax.ShapeDtypeStruct((rows, HD), F32)
    vmem = pl.BlockSpec(memory_space=pltpu.VMEM)
    dma = pltpu.SemaphoreType.DMA

    def room(*lead):
        return pltpu.VMEM(lead + (rows, HD), BF16)

    return pl.pallas_call(
        scatter_kernel,
        out_shape=(one, one),
        in_specs=[vmem] * 2,
        out_specs=(vmem, vmem),
        scratch_shapes=[
            room(4, 4, NX), room(4, 2, NZ), room(4, 4), room(NX, NY), room(NY, NZ), room(3, NY),
            room(NY), room(NY), room(2),
            dma((4, 4)), dma((4, 4)), dma((4, 2)), dma((4, 2)), dma((4, 4)), dma((4, 4)),
            dma((3,)), dma((3,)), dma((2,)), dma((2,)),
        ],
        compiler_params=pltpu.CompilerParams(
            collective_id=identity, has_side_effects=True, vmem_limit_bytes=32 * 2**20
        ),
        name=name,
    )(a_parts, b_parts)


def matmul(left, right, left_dim, right_dim):
    return lax.dot_general(
        left, right, (((left_dim,), (right_dim,)), ((), ())), preferred_element_type=F32
    )


def attention_kernel(q_ref, k_ref, v_ref, do_ref, o_ref, dq_ref, dk_ref, dv_ref, weights):
    length = q_ref.shape[0]
    heads = q_ref.shape[1] // HD
    columns = heads * length
    rank = lax.axis_index("context")
    first = rank * length
    full = first // TILE
    scale = HD ** (-0.5)
    factor = scale * LOG2E

    def stack(ref):
        return jnp.concatenate([ref[:, h * HD : (h + 1) * HD] for h in range(heads)], axis=0)

    queries = stack(q_ref)
    last_rows = pl.ds(pl.multiple_of(full * TILE, TILE), TILE)

    def rows_of(index):
        return pl.ds(pl.multiple_of(index * TILE, TILE), TILE)

    key_at = full * TILE + lax.broadcasted_iota(jnp.int32, (TILE, columns), 0)
    query_at = first + lax.rem(lax.broadcasted_iota(jnp.int32, (TILE, columns), 1), length)
    visible = key_at <= query_at

    def scores(rows):
        return matmul(k_ref[rows, :], queries, 1, 1)

    def max_step(index, current):
        return jnp.maximum(current, jnp.max(scores(rows_of(index)), axis=0, keepdims=True))

    top = jnp.max(jnp.where(visible, scores(last_rows), NEGATIVE), axis=0, keepdims=True)
    top = lax.fori_loop(0, full, max_step, top)
    top = top * factor

    def weigh(rows, current, masked):
        totals, output = current
        exponent = scores(rows) * factor - top
        if masked:
            exponent = jnp.where(visible, exponent, NEGATIVE)
        weight = jnp.exp2(exponent)
        totals = totals + jnp.sum(weight, axis=0, keepdims=True)
        low = weight.astype(BF16)
        weights[rows, :] = low
        return totals, output + matmul(v_ref[rows, :], low, 0, 0)

    start = (jnp.zeros((1, columns), F32), jnp.zeros((HD, columns), F32))
    start = weigh(last_rows, start, True)
    totals, output = lax.fori_loop(
        0, full, lambda index, current: weigh(rows_of(index), current, False), start
    )
    inverse = 1.0 / totals
    output = (output * inverse).astype(BF16).astype(F32)
    cotangent = stack(do_ref).astype(F32).T
    delta = jnp.sum(cotangent * output, axis=0, keepdims=True) * inverse
    scaled = cotangent * inverse
    scaled_across = scaled.astype(BF16)
    scaled_rows = scaled.T.astype(BF16)
    output_rows = output.T.astype(BF16)
    for h in range(heads):
        o_ref[:, h * HD : (h + 1) * HD] = output_rows[h * length : (h + 1) * length]

    def back(index, query_grad):
        rows = rows_of(index)
        low = weights[rows, :]
        change = matmul(v_ref[rows, :], scaled_across, 1, 0) - delta
        score_grad = (low.astype(F32) * change).astype(BF16)
        dk_ref[rows, :] = (matmul(score_grad, queries, 1, 0) * scale).astype(BF16)
        dv_ref[rows, :] = matmul(low, scaled_rows, 1, 0).astype(BF16)
        return query_grad + matmul(k_ref[rows, :], score_grad, 0, 0)

    query_grad = lax.fori_loop(0, full + 1, back, jnp.zeros((HD, columns), F32))
    grad_rows = query_grad.T * scale
    for h in range(heads):
        dq_ref[:, h * HD : (h + 1) * HD] = grad_rows[h * length : (h + 1) * length]

    @pl.loop(full + 1, k_ref.shape[0] // TILE)
    def _(index):
        rows = rows_of(index)
        dk_ref[rows, :] = jnp.zeros((TILE, HD), BF16)
        dv_ref[rows, :] = jnp.zeros((TILE, HD), BF16)


def attention(queries, keys, values, cotangent):
    length, width = queries.shape
    tokens = keys.shape[0]
    vmem = pl.BlockSpec(memory_space=pltpu.VMEM)
    columns = width // HD * length
    return pl.pallas_call(
        attention_kernel,
        out_shape=(
            jax.ShapeDtypeStruct((length, width), BF16),
            jax.ShapeDtypeStruct((length, width), F32),
            jax.ShapeDtypeStruct((tokens, HD), BF16),
            jax.ShapeDtypeStruct((tokens, HD), BF16),
        ),
        in_specs=[vmem] * 4,
        out_specs=(vmem,) * 4,
        scratch_shapes=[pltpu.VMEM((tokens, columns), BF16)],
        compiler_params=pltpu.CompilerParams(vmem_limit_bytes=48 * 2**20),
        cost_estimate=pl.CostEstimate(
            flops=14 * tokens * columns * HD, bytes_accessed=9 * 2**20, transcendentals=tokens * columns
        ),
        name="attention",
    )(queries, keys, values, cotangent)


def rope_tables(positions, head_width):
    half_width = head_width // 2
    exponent = jnp.arange(half_width, dtype=F32) * (2.0 / head_width)
    frequency = jnp.power(jnp.float32(THETA), -exponent)
    angles = positions.astype(F32)[:, None] * frequency[None, :]
    return (jnp.cos(angles), jnp.sin(angles))


def rotate(field, cosine_table, sine_table):
    half_width = field.shape[-1] // 2
    first_half = field[..., :half_width]
    second_half = field[..., half_width:]
    cosine_part = cosine_table[:, None, :]
    sine_part = sine_table[:, None, :]
    return jnp.concatenate(
        [
            first_half * cosine_part - second_half * sine_part,
            second_half * cosine_part + first_half * sine_part,
        ],
        axis=-1,
    )


def shards(hidden_in, value_first, w_query, w_key, w_value, w_out, value_mix, grad_out):
    tensor_count = lax.axis_size("tensor")
    context_rank = lax.axis_index("context")
    length, model_width = hidden_in.shape[1:]
    heads = w_query.shape[1] // HD
    share_rows = length // tensor_count
    inputs = hidden_in.reshape(length, model_width)
    firsts = value_first.reshape(length, HD)
    block_rows = context_rank * length + jnp.arange(length, dtype=jnp.int32)
    cosines, sines = rope_tables(block_rows, HD)

    def turned(field, sine_table):
        count = field.shape[1] // HD
        return (
            rotate(field.reshape(length, count, HD), cosines, sine_table)
            .astype(BF16)
            .reshape(length, count * HD)
        )

    keys = turned(jnp.dot(inputs, w_key, preferred_element_type=F32), sines)
    projected = jnp.dot(inputs, w_value, preferred_element_type=F32)
    mixed = (value_mix[0] * projected + value_mix[1] * firsts.astype(F32)).astype(BF16)
    keys_all, values_all = gather_blocks(keys, mixed)
    queries = turned(jnp.dot(inputs, w_query, preferred_element_type=F32), sines)
    grads = lax.all_gather(grad_out, "tensor", axis=1, tiled=True).reshape(length, model_width)
    cotangent = matmul(grads, w_out, 1, 1).astype(BF16)
    outputs, query_grad, key_parts, value_parts = attention(
        queries, keys_all.reshape(-1, HD), values_all.reshape(-1, HD), cotangent
    )
    attn_out = lax.psum_scatter(
        jnp.dot(outputs, w_out, preferred_element_type=F32).astype(BF16),
        "tensor",
        scatter_dimension=0,
        tiled=True,
    ).reshape(1, share_rows, model_width)
    blocks = (NY, NX, NZ, length, HD)
    key_sum, value_sum = scatter_blocks(
        key_parts.reshape(blocks), value_parts.reshape(blocks), 2, "scatter_grads"
    )
    query_pre = turned(query_grad, -sines)
    key_pre = turned(key_sum, -sines)
    value_pre = (value_mix[0] * value_sum).astype(BF16)
    first_grad = (value_mix[1] * value_sum).astype(BF16).reshape(1, length, HD)
    summed = matmul(query_pre, w_query, 1, 1)
    summed = summed + matmul(key_pre, w_key, 1, 1)
    grad_in = lax.psum_scatter(
        (summed + matmul(value_pre, w_value, 1, 1)).astype(BF16),
        "tensor",
        scatter_dimension=0,
        tiled=True,
    ).reshape(1, share_rows, model_width)
    strips = (NY, NX, NZ, model_width // (NY * NX * NZ), HD)
    key_weight, value_weight = scatter_blocks(
        matmul(inputs, key_pre, 0, 0).astype(BF16).reshape(strips),
        matmul(inputs, value_pre, 0, 0).astype(BF16).reshape(strips),
        3,
        "scatter_weights",
    )
    return (attn_out, grad_in, first_grad, key_weight, value_weight)


def solution(mesh):
    return jax.shard_map(
        shards,
        mesh=mesh,
        in_specs=(
            P("context", None, None),
            P("context", None, "tensor"),
            P(None, "tensor"),
            P(None, "tensor"),
            P(None, "tensor"),
            P("tensor", None),
            P(None, "tensor"),
            P("context", "tensor", None),
        ),
        out_specs=(
            P("context", "tensor", None),
            P("context", "tensor", None),
            P("context", None, "tensor"),
            P("context", "tensor"),
            P("context", "tensor"),
        ),
        check_vma=False,
    )
```

```python
import jax
import jax.numpy as jnp
from jax import lax
from jax.experimental import pallas as pl
from jax.experimental.pallas import tpu as pltpu
from jax.sharding import PartitionSpec as P

HD = 128
THETA = 500000.0
LOG2E = 1.4426950408889634
NEGATIVE = -1e30
NY, NX, NZ = 2, 4, 8
NH = NZ // 2
F32, BF16 = jnp.float32, jnp.bfloat16

CHAINS = ((1, 0, 4, 2), (1, 1, 3, 1), (-1, 1, 4, 2), (-1, 0, 3, 1))
ORDER = (0, 2, 1, 3)
ARRIVE = ((0, 3), (1, 2))


def rank_of(y, x, z):
    return (y * NX + x) * NZ + z


def turn(value, step, count):
    return lax.rem(value + (step + count), count)


def when(condition, action):
    if condition is True:
        action()
    else:
        pl.when(condition)(action)


def matmul(left, right, left_dim, right_dim):
    return lax.dot_general(
        left, right, (((left_dim,), (right_dim,)), ((), ())), preferred_element_type=F32
    )


def add_into(target, term):
    target[...] = (target[...].astype(F32) + term[...].astype(F32)).astype(BF16)


class Sender:
    def __init__(self):
        self.started = []

    def build(self, source, target, send_sem, recv_sem, axis, rank):
        return pltpu.make_async_remote_copy(
            src_ref=source,
            dst_ref=target,
            send_sem=send_sem,
            recv_sem=recv_sem,
            device_id={axis: rank},
            device_id_type=pl.DeviceIdType.MESH,
        )

    def go(self, copy, condition=True):
        copy.start()
        self.started.append((condition, copy))
        return copy

    def finish(self):
        for condition, copy in self.started:
            when(condition, copy.wait_send)


def gather_steps(send, place, k_own, v_own, k_all, v_all, sems):
    y, x, z, holder = place
    y_send, y_recv, kx_send, kx_recv, vz_send, vz_recv, kz_send, kz_recv, vx_send, vx_recv = sems
    slot = z // 2
    partner = rank_of(1 - y, x, z)
    lends = jnp.logical_not(holder(z))
    pairs = [
        send.build(own, whole.at[y, x, slot], y_send.at[i], y_recv.at[i], "context", partner)
        for i, (own, whole) in enumerate(((k_own, k_all), (v_own, v_all)))
    ]

    def lend():
        for copy in pairs:
            copy.start()

    def keep():
        k_all[y, x, slot] = k_own[...]
        v_all[y, x, slot] = v_own[...]

    pl.when(lends)(lend)
    pl.when(holder(z))(keep)
    send.started += [(lends, copy) for copy in pairs]

    kx = []
    for step in (1, 2, 3):
        part = k_all.at[:, x, slot]
        kx.append(
            send.build(
                part, part, kx_send.at[step - 1], kx_recv.at[step - 1], "context",
                rank_of(y, turn(x, step, NX), z),
            )
        )

    def z_hop(chain, hop, whole, lead, send_sem, recv_sem):
        way, half, _, _ = CHAINS[chain]
        origin = turn(z, -way * hop, NZ)
        part = whole.at[half, lead, origin // 2]
        copy = send.build(
            part, part, send_sem.at[chain, hop], recv_sem.at[chain, hop], "context",
            rank_of(y, x, turn(z, way, NZ)),
        )
        return holder(origin), copy

    def vz_hop(chain, hop):
        return z_hop(chain, hop, v_all, x, vz_send, vz_recv)

    def kz_hop(chain, hop):
        return z_hop(chain, hop, k_all, slice(None), kz_send, kz_recv)

    def vx_hop(chain, hop):
        way, half, _, _ = CHAINS[chain]
        part = v_all.at[half, turn(x, -way * hop, NX)]
        return True, send.build(
            part, part, vx_send.at[chain, hop], vx_recv.at[chain, hop], "context",
            rank_of(y, turn(x, way, NX), z),
        )

    def advance(hop_of, hop, ring):
        for chain in ORDER:
            if hop < CHAINS[chain][ring]:
                condition, copy = hop_of(chain, hop)

                def act():
                    if hop:
                        hop_of(chain, hop - 1)[1].wait_recv()
                    copy.start()

                when(condition, act)
                send.started.append((condition, copy))

    def drain(hop_of, ring, parity):
        for chain in ORDER:
            hops = CHAINS[chain][ring]
            condition = True
            if parity:
                condition = holder(turn(z, -CHAINS[chain][0] * hops, NZ))
            when(condition, hop_of(chain, hops - 1)[1].wait_recv)

    yield

    def pair_keys():
        pairs[0].wait_recv()
        for copy in kx:
            copy.start()
        pairs[1].wait_recv()

    pl.when(holder(z))(pair_keys)
    send.started += [(holder(z), copy) for copy in kx]
    advance(vz_hop, 0, 2)

    def row_keys():
        for copy in kx:
            copy.wait_recv()

    pl.when(holder(z))(row_keys)
    advance(kz_hop, 0, 2)
    advance(vz_hop, 1, 2)
    advance(vz_hop, 2, 2)
    advance(kz_hop, 1, 2)
    yield
    advance(vz_hop, 3, 2)
    drain(vz_hop, 2, True)
    advance(vx_hop, 0, 3)
    advance(kz_hop, 2, 2)
    yield
    advance(kz_hop, 3, 2)
    advance(vx_hop, 1, 3)
    yield
    drain(kz_hop, 2, True)
    drain(vx_hop, 3, False)
    yield


def scatter_steps(send, place, parity, a_in, b_in, a_out, b_out, bufs, sems):
    y, x, z, holder_of = place
    az_buf, bx_buf, bz_buf, a_sum, b_sum, ax_buf, low, y_buf = bufs
    az_send, az_recv, bx_send, bx_recv, bz_send, bz_recv, ax_send, ax_recv, y_send, y_recv = sems

    def holder(at):
        return holder_of(at) if parity else True

    def index(at):
        return at // 2 if parity else at

    def z_hop(chain, hop, own_of, buf, send_sem, recv_sem):
        way, half, hops, _ = CHAINS[chain]
        far = turn(z, way * (hops - hop), NZ)
        own = own_of(half, index(far))
        source = buf.at[chain, hop - 1] if hop else own
        copy = send.build(
            source, buf.at[chain, hop], send_sem.at[chain, hop], recv_sem.at[chain, hop],
            "context", rank_of(y, x, turn(z, way, NZ)),
        )
        return holder(far), own, copy

    def az_hop(chain, hop):
        return z_hop(chain, hop, lambda half, at: a_in.at[half, :, at], az_buf, az_send, az_recv)

    def bz_hop(chain, hop):
        return z_hop(chain, hop, lambda half, at: b_sum.at[half, at], bz_buf, bz_send, bz_recv)

    def bx_hop(chain, hop):
        way, half, _, hops = CHAINS[chain]
        own = b_in.at[half, turn(x, way * (hops - hop), NX)]
        source = bx_buf.at[chain, hop - 1] if hop else own
        copy = send.build(
            source, bx_buf.at[chain, hop], bx_send.at[chain, hop], bx_recv.at[chain, hop],
            "context", rank_of(y, turn(x, way, NX), z),
        )
        return True, own, copy

    def advance(hop_of, buf, hop, ring):
        for chain in ORDER:
            if hop < CHAINS[chain][ring]:
                condition, own, copy = hop_of(chain, hop)

                def act():
                    if hop:
                        hop_of(chain, hop - 1)[2].wait_recv()
                        add_into(buf.at[chain, hop - 1], own)
                    copy.start()

                when(condition, act)
                send.started.append((condition, copy))

    def drain(hop_of, ring):
        for chain in ORDER:
            hop_of(chain, CHAINS[chain][ring] - 1)[2].wait_recv()

    def total(own, buf, half, ring):
        right, left = ARRIVE[half]
        return (
            own.astype(F32)
            + buf[right, CHAINS[right][ring] - 1].astype(F32)
            + buf[left, CHAINS[left][ring] - 1].astype(F32)
        )

    partner = rank_of(1 - y, x, z)
    pairs = [
        send.build(
            low.at[i, 1 - y], y_buf.at[i], y_send.at[i], y_recv.at[i], "context", partner
        )
        for i in range(2)
    ]

    def hand_over(i, out):
        if parity:
            pl.when(holder(z))(pairs[i].start)
            send.started.append((holder(z), pairs[i]))
        else:
            send.go(pairs[i])

    def close(i, out):
        if parity:

            def keep():
                out[...] = low[i, y].astype(F32)

            def take():
                pairs[i].wait_recv()
                out[...] = y_buf[i].astype(F32)

            pl.when(holder(z))(keep)
            pl.when(jnp.logical_not(holder(z)))(take)
        else:
            pairs[i].wait_recv()
            out[...] = low[i, y].astype(F32) + y_buf[i].astype(F32)

    advance(az_hop, az_buf, 0, 2)
    advance(bx_hop, bx_buf, 0, 3)
    yield
    advance(az_hop, az_buf, 1, 2)
    advance(bx_hop, bx_buf, 1, 3)
    yield
    advance(az_hop, az_buf, 2, 2)
    drain(bx_hop, 3)
    for half in range(NY):
        b_sum[half] = total(b_in[half, x], bx_buf, half, 3).astype(BF16)
    advance(bz_hop, bz_buf, 0, 2)
    advance(az_hop, az_buf, 3, 2)
    advance(bz_hop, bz_buf, 1, 2)
    ax = []
    for step in (1, 2, 3):
        other = turn(x, step, NX)
        ax.append(
            send.build(
                a_sum.at[other], ax_buf.at[step - 1], ax_send.at[step - 1], ax_recv.at[step - 1],
                "context", rank_of(y, other, z),
            )
        )

    def a_ring():
        drain(az_hop, 2)
        for half in range(NY):
            a_sum[:, half] = total(a_in[half, :, index(z)], az_buf, half, 2).astype(BF16)
        for copy in ax:
            copy.start()

    when(holder(z), a_ring)
    send.started += [(holder(z), copy) for copy in ax]
    yield
    advance(bz_hop, bz_buf, 2, 2)

    def a_row():
        for copy in ax:
            copy.wait_recv()
        summed = a_sum[x].astype(F32)
        for step in range(3):
            summed = summed + ax_buf[step].astype(F32)
        low[0] = summed.astype(BF16)

    when(holder(z), a_row)
    hand_over(0, a_out)
    advance(bz_hop, bz_buf, 3, 2)
    yield

    def b_ring():
        drain(bz_hop, 2)
        for half in range(NY):
            low[1, half] = total(b_sum[half, index(z)], bz_buf, half, 2).astype(BF16)

    when(holder(z), b_ring)
    hand_over(1, b_out)
    close(0, a_out)
    close(1, b_out)
    yield


def block_kernel(
    x_hbm, first_ref, wq_hbm, wk_hbm, wv_hbm, wo_hbm, mix_ref, g_hbm, cos_ref, sin_ref,
    attn_ref, gin_ref, gfirst_ref, gwk_ref, gwv_ref,
    x_buf, wq, wk, wv, wo, g_all, xt, k_own, v_own, k_all, v_all, q_all, cot_all, weights,
    o_acc, dq_acc, o_send, o_recv, dq_send, dq_recv, stat_mine, stat_pair, dk_all, dv_all,
    k_sum, v_sum, part_out, recv_out, part_in, recv_in, acc_in, wk_part, wv_part,
    grad_bufs, weight_bufs, local_sem, gather_sems, grad_sems, weight_sems,
    pair_send, pair_recv, g_send, g_recv, out_send, out_recv, in_send, in_recv,
):
    rank = lax.axis_index("context")
    y, x, z = rank // (NX * NZ), (rank // NZ) % NX, rank % NZ
    tensor, tensors = lax.axis_index("tensor"), lax.axis_size("tensor")
    length, width = x_buf.shape
    columns = q_all.shape[1]
    heads = columns // length
    share = length // tensors
    tile = NH * length
    scale = HD ** (-0.5)
    factor = scale * LOG2E

    def holder(at):
        return lax.rem(at + y, 2) == 0

    place = (y, x, z, holder)
    other = rank_of(1 - y, NX - 1 - x, NZ - 1 - z)
    peers = [lax.rem(tensor + step, tensors) for step in range(1, tensors)]
    my_rows = pl.ds(pl.multiple_of(tensor * share, share), share)

    loads = [
        pltpu.make_async_copy(source, target, local_sem.at[i])
        for i, (source, target) in enumerate(
            ((x_hbm, x_buf), (wk_hbm, wk), (wv_hbm, wv), (g_hbm, g_all.at[my_rows]), (wq_hbm, wq),
             (wo_hbm, wo))
        )
    ]
    for copy in loads:
        copy.start()
    barrier = pltpu.get_barrier_semaphore()
    ranks = [rank_of(1 - y, x, z), rank_of(y, x, turn(z, 1, NZ)), rank_of(y, x, turn(z, -1, NZ))]
    ranks += [rank_of(y, turn(x, step, NX), z) for step in (1, 2, 3)]
    ranks += [other]
    for who in [{"context": at} for at in ranks] + [{"tensor": at} for at in peers]:
        pl.semaphore_signal(barrier, inc=1, device_id=who, device_id_type=pl.DeviceIdType.MESH)

    cosines, sines = cos_ref[...], sin_ref[...]

    def spread(table):
        return jnp.concatenate([table] * heads, axis=0)

    def swap(field):
        return jnp.concatenate([field[:, HD // 2 :], field[:, : HD // 2]], axis=1)

    def rot(field, cosine_part, sine_part):
        return field * cosine_part + swap(field) * sine_part

    def stack(field):
        return jnp.concatenate([field[:, h * HD : (h + 1) * HD] for h in range(heads)], axis=0)

    def unstack(field):
        return jnp.concatenate(
            [field[h * length : (h + 1) * length] for h in range(heads)], axis=1
        )

    for copy in loads[:3]:
        copy.wait()
    inputs = x_buf[...]
    k_own[...] = rot(matmul(inputs, wk[...], 1, 0), cosines, sines).astype(BF16)
    v_own[...] = (
        mix_ref[0, 0] * matmul(inputs, wv[...], 1, 0) + mix_ref[1, 0] * first_ref[...].astype(F32)
    ).astype(BF16)
    pl.semaphore_wait(barrier, len(ranks) + len(peers))

    send = Sender()
    gather = gather_steps(send, place, k_own, v_own, k_all, v_all, gather_sems)
    next(gather)
    loads[3].wait()
    g_copies = [
        send.go(
            send.build(
                g_all.at[my_rows], g_all.at[my_rows], g_send.at[i], g_recv.at[i], "tensor", peer
            )
        )
        for i, peer in enumerate(peers)
    ]
    next(gather)
    loads[4].wait()
    q_all[y] = rot(
        stack(matmul(x_buf[...], wq[...], 1, 0)), spread(cosines), spread(sines)
    ).astype(BF16)
    pair_q = send.go(
        send.build(q_all.at[y], q_all.at[y], pair_send.at[0], pair_recv.at[0], "context", other)
    )
    next(gather)
    for copy in g_copies:
        copy.wait_recv()
    loads[5].wait()
    for h in range(heads):
        cot_all[y, :, h * length : (h + 1) * length] = matmul(
            wo[h * HD : (h + 1) * HD, :], g_all[...], 1, 1
        ).astype(BF16)
    pair_cot = send.go(
        send.build(cot_all.at[y], cot_all.at[y], pair_send.at[1], pair_recv.at[1], "context", other)
    )
    next(gather)
    xt[...] = x_buf[...].T
    dk_all[...] = jnp.zeros(dk_all.shape, BF16)
    dv_all[...] = jnp.zeros(dv_all.shape, BF16)
    next(gather)
    pair_q.wait_recv()
    pair_cot.wait_recv()

    key_in_tile = lax.broadcasted_iota(jnp.int32, (tile, columns), 0)
    key_in_tile = (2 * (key_in_tile // length) + y) * length + lax.rem(key_in_tile, length)
    query_in_block = lax.rem(lax.broadcasted_iota(jnp.int32, (tile, columns), 1), length)
    low_rank = jnp.minimum(rank, NY * NX * NZ - 1 - rank)

    def block_of(slot):
        return jnp.where(slot == 0, low_rank, NY * NX * NZ - 1 - low_rank)

    def tile_of(ref, row):
        return ref[row // NX, lax.rem(row, NX)].reshape(tile, HD)

    @pl.loop(0, 2)
    def _(slot):
        block = block_of(slot)
        last = block // NZ
        visible = key_in_tile <= query_in_block + lax.rem(block, NZ) * length
        queries = q_all[slot]

        def scores(row):
            return matmul(tile_of(k_all, row), queries, 1, 1)

        def max_step(row, current):
            return jnp.maximum(current, jnp.max(scores(row), axis=0, keepdims=True))

        top = jnp.max(jnp.where(visible, scores(last), NEGATIVE), axis=0, keepdims=True)
        top = lax.fori_loop(0, last, max_step, top) * factor

        def weigh(row, current, masked):
            totals, output = current
            exponent = scores(row) * factor - top
            if masked:
                exponent = jnp.where(visible, exponent, NEGATIVE)
            weight = jnp.exp2(exponent)
            totals = totals + jnp.sum(weight, axis=0, keepdims=True)
            low = weight.astype(BF16)
            weights[slot * NX + row] = low
            return totals, output + matmul(tile_of(v_all, row), low, 0, 0)

        start = (jnp.zeros((1, columns), F32), jnp.zeros((HD, columns), F32))
        start = weigh(last, start, True)
        totals, output = lax.fori_loop(
            0, last, lambda row, current: weigh(row, current, False), start
        )
        delta = jnp.sum(cot_all[slot].astype(F32) * output, axis=0, keepdims=True)
        stat_mine[slot, 0:1] = top
        stat_mine[slot, 1:2] = totals
        stat_mine[slot, 2:3] = delta
        o_acc[slot] = output

    pair_stat = send.go(
        send.build(stat_mine, stat_pair, pair_send.at[2], pair_recv.at[2], "context", other)
    )
    o_send[...] = o_acc[1 - y].astype(BF16)
    pair_o = send.go(
        send.build(o_send, o_recv, pair_send.at[3], pair_recv.at[3], "context", other)
    )
    pair_stat.wait_recv()

    def merged(slot):
        top = jnp.maximum(stat_mine[slot, 0:1], stat_pair[slot, 0:1])
        mine = jnp.exp2(stat_mine[slot, 0:1] - top)
        theirs = jnp.exp2(stat_pair[slot, 0:1] - top)
        inverse = 1.0 / (stat_mine[slot, 1:2] * mine + stat_pair[slot, 1:2] * theirs)
        return mine * inverse, theirs * inverse

    @pl.loop(0, 2)
    def _(step):
        slot = 1 - step
        mine, theirs = merged(slot)
        delta = (stat_mine[slot, 2:3] * mine + stat_pair[slot, 2:3] * theirs) * mine
        scaled = cot_all[slot].astype(F32) * mine
        scaled_across = scaled.astype(BF16)
        scaled_rows = scaled.T.astype(BF16)
        queries = q_all[slot]

        def back(row, query_grad):
            low = weights[slot * NX + row]
            change = matmul(tile_of(v_all, row), scaled_across, 1, 0) - delta
            score_grad = (low.astype(F32) * change).astype(BF16)
            key_term = matmul(score_grad, queries, 1, 0) * scale
            value_term = matmul(low, scaled_rows, 1, 0)
            shape = (NH, length, HD)
            at = (row // NX, lax.rem(row, NX))
            dk_all[at] = (dk_all[at].astype(F32) + key_term.reshape(shape)).astype(BF16)
            dv_all[at] = (dv_all[at].astype(F32) + value_term.reshape(shape)).astype(BF16)
            return query_grad + matmul(tile_of(k_all, row), score_grad, 0, 0)

        dq_acc[slot] = lax.fori_loop(
            0, block_of(slot) // NZ + 1, back, jnp.zeros((HD, columns), F32)
        )

    scatter = scatter_steps(
        send, place, True, dk_all, dv_all, k_sum, v_sum, grad_bufs, grad_sems
    )
    next(scatter)
    dq_send[...] = dq_acc[1 - y].astype(BF16)
    pair_dq = send.go(
        send.build(dq_send, dq_recv, pair_send.at[4], pair_recv.at[4], "context", other)
    )

    def share_out(part, recv, send_sem, recv_sem):
        return [
            send.go(
                send.build(
                    part.at[peer], recv.at[i], send_sem.at[i], recv_sem.at[i], "tensor", peer
                )
            )
            for i, peer in enumerate(peers)
        ]

    def add_up(part, recv, copies, out):
        for copy in copies:
            copy.wait_recv()
        summed = part[tensor].astype(F32)
        for i in range(len(copies)):
            summed = summed + recv[i].astype(F32)
        out[...] = summed.astype(BF16)

    strip = min(512, width)

    def strip_of(index):
        return pl.ds(pl.multiple_of(index * strip, strip), strip)

    pair_o.wait_recv()
    mine, theirs = merged(y)
    outputs = unstack(
        (o_acc[y] * mine + o_recv[...].astype(F32) * theirs).T.astype(BF16)
    )

    @pl.loop(0, width // strip)
    def _(index):
        at = strip_of(index)
        term = matmul(outputs, wo[:, at], 1, 0).astype(BF16)
        for peer in range(tensors):
            part_out[peer, :, at] = term[peer * share : (peer + 1) * share]

    out_copies = share_out(part_out, recv_out, out_send, out_recv)
    next(scatter)
    pair_dq.wait_recv()
    query_pre = unstack(
        rot(
            (dq_acc[y] + dq_recv[...].astype(F32)).T * scale, spread(cosines), -spread(sines)
        ).astype(BF16)
    )

    @pl.loop(0, width // strip)
    def _(index):
        at = strip_of(index)
        acc_in[:, at] = matmul(query_pre, wq[at, :], 1, 1)

    next(scatter)
    next(scatter)
    add_up(part_out, recv_out, out_copies, attn_ref)
    next(scatter)
    key_pre = rot(k_sum[...], cosines, -sines).astype(BF16)
    value_sum = v_sum[...]
    value_pre = (mix_ref[0, 0] * value_sum).astype(BF16)
    strips = wk_part.shape
    wk_part[...] = matmul(xt[...], key_pre, 1, 0).astype(BF16).reshape(strips)
    wv_part[...] = matmul(xt[...], value_pre, 1, 0).astype(BF16).reshape(strips)
    scatter = scatter_steps(
        send, place, False, wk_part, wv_part, gwk_ref, gwv_ref, weight_bufs, weight_sems
    )
    next(scatter)
    gfirst_ref[...] = (mix_ref[1, 0] * value_sum).astype(BF16)

    @pl.loop(0, width // strip)
    def _(index):
        at = strip_of(index)
        term = acc_in[:, at] + matmul(key_pre, wk[at, :], 1, 1)
        term = (term + matmul(value_pre, wv[at, :], 1, 1)).astype(BF16)
        for peer in range(tensors):
            part_in[peer, :, at] = term[peer * share : (peer + 1) * share]

    in_copies = share_out(part_in, recv_in, in_send, in_recv)
    for _ in range(3):
        next(scatter)
    add_up(part_in, recv_in, in_copies, gin_ref)
    next(scatter)
    send.finish()


def rope_tables(positions, head_width):
    half_width = head_width // 2
    exponent = jnp.arange(half_width, dtype=F32) * (2.0 / head_width)
    frequency = jnp.power(jnp.float32(THETA), -exponent)
    angles = positions.astype(F32)[:, None] * frequency[None, :]
    return (jnp.cos(angles), jnp.sin(angles))


def shards(hidden_in, value_first, w_query, w_key, w_value, w_out, value_mix, grad_out):
    tensors = lax.axis_size("tensor")
    length, width = hidden_in.shape[1:]
    features = w_query.shape[1]
    columns = features // HD * length
    share = length // tensors
    rows = width // (NY * NX * NZ)
    block_rows = lax.axis_index("context") * length + jnp.arange(length, dtype=jnp.int32)
    cosines, sines = rope_tables(block_rows, HD)
    cosines = jnp.concatenate([cosines, cosines], axis=1)
    sines = jnp.concatenate([-sines, sines], axis=1)
    vmem = pl.BlockSpec(memory_space=pltpu.VMEM)
    hbm = pl.BlockSpec(memory_space=pl.ANY)
    smem = pl.BlockSpec(memory_space=pltpu.SMEM)
    dma = pltpu.SemaphoreType.DMA

    def low(*shape):
        return pltpu.VMEM(shape, BF16)

    def full(*shape):
        return pltpu.VMEM(shape, F32)

    def scatter_room(ends, count):
        return (
            low(4, 4, NX, count, HD), low(4, 2, ends, count, HD), low(4, 4, count, HD),
            low(NX, NY, count, HD), low(NY, ends, count, HD), low(3, NY, count, HD),
            low(2, NY, count, HD), low(2, count, HD),
        )

    others = (max(tensors - 1, 1),)
    scratch = [
        low(length, width), low(width, features), low(width, HD), low(width, HD),
        low(features, width), low(length, width), low(width, length), low(length, HD),
        low(length, HD), low(NY, NX, NH, length, HD), low(NY, NX, NH, length, HD),
        low(2, columns, HD), low(2, HD, columns), low(3 * NX, NH * length, columns),
        full(2, HD, columns), full(2, HD, columns), low(HD, columns), low(HD, columns),
        low(HD, columns), low(HD, columns), full(2, 8, columns), full(2, 8, columns),
        low(NY, NX, NH, length, HD), low(NY, NX, NH, length, HD), full(length, HD),
        full(length, HD), low(tensors, share, width), low(others[0], share, width),
        low(tensors, share, width), low(others[0], share, width), full(length, width),
        low(NY, NX, NZ, rows, HD), low(NY, NX, NZ, rows, HD),
        scatter_room(NH, length), scatter_room(NZ, rows), dma((6,)),
        (dma((2,)), dma((2,)), dma((3,)), dma((3,)), dma((4, 4)), dma((4, 4)), dma((4, 4)),
         dma((4, 4)), dma((4, 2)), dma((4, 2))),
    ]
    scatter_sems = (
        dma((4, 4)), dma((4, 4)), dma((4, 2)), dma((4, 2)), dma((4, 4)), dma((4, 4)), dma((3,)),
        dma((3,)), dma((2,)), dma((2,)),
    )
    scratch += [scatter_sems, scatter_sems, dma((5,)), dma((5,))] + [dma(others)] * 6
    attn_out, grad_in, grad_first, key_weight, value_weight = pl.pallas_call(
        block_kernel,
        out_shape=(
            jax.ShapeDtypeStruct((share, width), BF16),
            jax.ShapeDtypeStruct((share, width), BF16),
            jax.ShapeDtypeStruct((length, HD), BF16),
            jax.ShapeDtypeStruct((rows, HD), F32),
            jax.ShapeDtypeStruct((rows, HD), F32),
        ),
        in_specs=[hbm, vmem, hbm, hbm, hbm, hbm, smem, hbm, vmem, vmem],
        out_specs=(vmem,) * 5,
        scratch_shapes=scratch,
        compiler_params=pltpu.CompilerParams(
            collective_id=1, has_side_effects=True, vmem_limit_bytes=56 * 2**20
        ),
        name="attention_block",
    )(
        hidden_in.reshape(length, width), value_first.reshape(length, HD), w_query, w_key, w_value,
        w_out, value_mix, grad_out.reshape(share, width), cosines, sines,
    )
    return (
        attn_out.reshape(1, share, width),
        grad_in.reshape(1, share, width),
        grad_first.reshape(1, length, HD),
        key_weight,
        value_weight,
    )


def solution(mesh):
    return jax.shard_map(
        shards,
        mesh=mesh,
        in_specs=(
            P("context", None, None),
            P("context", None, "tensor"),
            P(None, "tensor"),
            P(None, "tensor"),
            P(None, "tensor"),
            P("tensor", None),
            P(None, "tensor"),
            P("context", "tensor", None),
        ),
        out_specs=(
            P("context", "tensor", None),
            P("context", "tensor", None),
            P("context", None, "tensor"),
            P("context", "tensor"),
            P("context", "tensor"),
        ),
        check_vma=False,
    )
```

```python
import jax
import jax.numpy as jnp
from jax import lax
from jax.experimental import pallas as pl
from jax.experimental.pallas import tpu as pltpu
from jax.sharding import PartitionSpec as P

HD = 128
THETA = 500000.0
LOG2E = 1.4426950408889634
NEGATIVE = -1e30
NY, NX, NZ = 2, 4, 8
NH = NZ // 2
F32, BF16 = jnp.float32, jnp.bfloat16

CHAINS = ((1, 0, 4, 2), (1, 1, 3, 1), (-1, 1, 4, 2), (-1, 0, 3, 1))
ORDER = (0, 2, 1, 3)
ARRIVE = ((0, 3), (1, 2))


def rank_of(y, x, z):
    return (y * NX + x) * NZ + z


def turn(value, step, count):
    return lax.rem(value + (step + count), count)


def when(condition, action):
    if condition is True:
        action()
    else:
        pl.when(condition)(action)


def matmul(left, right, left_dim, right_dim):
    return lax.dot_general(
        left, right, (((left_dim,), (right_dim,)), ((), ())), preferred_element_type=F32
    )


def add_into(target, term):
    target[...] = (target[...].astype(F32) + term[...].astype(F32)).astype(BF16)


class Sender:
    def __init__(self):
        self.started = []

    def build(self, source, target, send_sem, recv_sem, axis, rank):
        return pltpu.make_async_remote_copy(
            src_ref=source,
            dst_ref=target,
            send_sem=send_sem,
            recv_sem=recv_sem,
            device_id={axis: rank},
            device_id_type=pl.DeviceIdType.MESH,
        )

    def go(self, copy, condition=True):
        copy.start()
        self.started.append((condition, copy))
        return copy

    def finish(self):
        for condition, copy in self.started:
            when(condition, copy.wait_send)


def gather_steps(send, place, k_own, v_own, k_all, v_all, sems):
    y, x, z, holder = place
    y_send, y_recv, kx_send, kx_recv, vz_send, vz_recv, kz_send, kz_recv = sems[:8]
    vx_send, vx_recv, vf_send, vf_recv = sems[8:]
    slot = z // 2
    partner = rank_of(1 - y, x, z)
    lends = jnp.logical_not(holder(z))
    pairs = [
        send.build(own, whole.at[y, x, slot], y_send.at[i], y_recv.at[i], "context", partner)
        for i, (own, whole) in enumerate(((k_own, k_all), (v_own, v_all)))
    ]

    def lend():
        for copy in pairs:
            copy.start()

    def keep():
        k_all[y, x, slot] = k_own[...]
        v_all[y, x, slot] = v_own[...]

    pl.when(lends)(lend)
    pl.when(holder(z))(keep)
    send.started += [(lends, copy) for copy in pairs]

    kx = {}
    for step in (1, 3, 2):
        part = k_all.at[:, x, slot]
        kx[step] = send.build(
            part, part, kx_send.at[step - 1], kx_recv.at[step - 1], "context",
            rank_of(y, turn(x, step, NX), z),
        )
    rows = (0, 1, 3, 2)

    def kz_copy(chain, hop, part_at):
        way, half, _, _ = CHAINS[chain]
        part = k_all.at[half, turn(x, rows[part_at], NX), turn(z, -way * hop, NZ) // 2]
        return send.build(
            part, part, kz_send.at[chain, hop, part_at], kz_recv.at[chain, hop, part_at],
            "context", rank_of(y, x, turn(z, way, NZ)),
        )

    def kz(hop, part_at):
        if hop == 0 and part_at:
            pl.when(holder(z))(kx[NX - rows[part_at]].wait_recv)
        for chain in ORDER:
            if hop < CHAINS[chain][2]:
                condition = holder(turn(z, -CHAINS[chain][0] * hop, NZ))
                copy = kz_copy(chain, hop, part_at)

                def act():
                    if hop:
                        kz_copy(chain, hop - 1, part_at).wait_recv()
                    copy.start()

                when(condition, act)
                send.started.append((condition, copy))

    def vz_copy(chain, hop):
        way, half, _, _ = CHAINS[chain]
        part = v_all.at[half, x, turn(z, -way * hop, NZ) // 2]
        return send.build(
            part, part, vz_send.at[chain, hop], vz_recv.at[chain, hop], "context",
            rank_of(y, x, turn(z, way, NZ)),
        )

    def vx_copy(half, at, way):
        part = v_all.at[half, x, at]
        side = 0 if way > 0 else 1
        return send.build(
            part, part, vx_send.at[half, at, side], vx_recv.at[half, at, side], "context",
            rank_of(y, turn(x, way, NX), z),
        )

    def vf_copy(half, at):
        way = 1 if half == 0 else -1
        part = v_all.at[half, turn(x, -way, NX), at]
        return send.build(
            part, part, vf_send.at[half, at], vf_recv.at[half, at], "context",
            rank_of(y, turn(x, way, NX), z),
        )

    def pieces(distance):
        if distance == 0:
            return [(None, holder(z), half, slot) for half in range(NY)]
        found = []
        for chain in ORDER:
            way, half, hops, _ = CHAINS[chain]
            if distance <= hops:
                origin = turn(z, -way * distance, NZ)
                found.append((chain, holder(origin), half, origin // 2))
        return found

    def v_round(distance):
        for chain, condition, half, at in pieces(distance):
            copies = [vx_copy(half, at, 1), vx_copy(half, at, -1)]
            if chain is None:
                copies += [vz_copy(c, 0) for c in ORDER if CHAINS[c][1] == half]
            elif distance < CHAINS[chain][2]:
                copies.insert(0, vz_copy(chain, distance))

            def act():
                if chain is not None:
                    vz_copy(chain, distance - 1).wait_recv()
                for copy in copies:
                    copy.start()

            when(condition, act)
            send.started += [(condition, copy) for copy in copies]

    def forward(distance):
        for _, condition, half, at in pieces(distance):
            copy = vf_copy(half, at)

            def act():
                vx_copy(half, at, 1 if half == 0 else -1).wait_recv()
                copy.start()

            when(condition, act)
            send.started.append((condition, copy))

    def finish():
        for distance in range(5):
            for _, condition, half, at in pieces(distance):

                def act():
                    vx_copy(half, at, -1 if half == 0 else 1).wait_recv()
                    vf_copy(half, at).wait_recv()

                when(condition, act)
        for chain in ORDER:
            way, _, hops, _ = CHAINS[chain]
            condition = holder(turn(z, -way * hops, NZ))

            def act():
                for part_at in range(NX):
                    kz_copy(chain, hops - 1, part_at).wait_recv()

            when(condition, act)

    yield

    def start_rows():
        for copy in pairs:
            copy.wait_recv()
        for copy in kx.values():
            copy.start()

    pl.when(holder(z))(start_rows)
    send.started += [(holder(z), copy) for copy in kx.values()]
    v_round(0)
    kz(0, 0)
    v_round(1)
    kz(0, 1)
    kz(1, 0)
    forward(0)
    yield
    v_round(2)
    kz(0, 2)
    kz(1, 1)
    kz(2, 0)
    forward(1)
    yield
    v_round(3)
    kz(0, 3)
    kz(1, 2)
    kz(2, 1)
    kz(3, 0)
    forward(2)
    v_round(4)
    kz(1, 3)
    kz(2, 2)
    kz(3, 1)
    forward(3)
    kz(2, 3)
    kz(3, 2)
    forward(4)
    kz(3, 3)
    yield
    finish()
    yield


def fold_steps(send, place, parity, a_in, b_in, a_out, b_out, bufs, sems):
    y, x, z, holder_of = place

    def holder(at):
        return holder_of(at) if parity else True

    def index(at):
        return at // 2 if parity else at

    az_buf, far_buf, near_buf, bz_buf, a_sum, b_sum, ax_buf, low, y_buf = bufs
    az_send, az_recv, far_send, far_recv, near_send, near_recv, bz_send, bz_recv = sems[:8]
    ax_send, ax_recv, y_send, y_recv = sems[8:]
    slot = index(z)
    rows = (2, 1, 3, 0)

    def az_copy(chain, hop, part_at):
        way, half, hops, _ = CHAINS[chain]
        own = a_in.at[half, turn(x, rows[part_at], NX), index(turn(z, way * (hops - hop), NZ))]
        source = az_buf.at[chain, hop - 1, part_at] if hop else own
        copy = send.build(
            source, az_buf.at[chain, hop, part_at], az_send.at[chain, hop, part_at],
            az_recv.at[chain, hop, part_at], "context", rank_of(y, x, turn(z, way, NZ)),
        )
        return own, copy

    def az(hop, part_at):
        for chain in ORDER:
            way, _, hops, _ = CHAINS[chain]
            if hop < hops:
                condition = holder(turn(z, way * (hops - hop), NZ))
                own, copy = az_copy(chain, hop, part_at)

                def act():
                    if hop:
                        az_copy(chain, hop - 1, part_at)[1].wait_recv()
                        add_into(az_buf.at[chain, hop - 1, part_at], own)
                    copy.start()

                when(condition, act)
                send.started.append((condition, copy))

    def ax_copy(step):
        goal = turn(x, step, NX)
        return send.build(
            a_sum.at[goal], ax_buf.at[step - 1], ax_send.at[step - 1], ax_recv.at[step - 1],
            "context", rank_of(y, goal, z),
        )

    def a_end(part_at):
        row = turn(x, rows[part_at], NX)

        def act():
            for half in range(NY):
                summed = a_in[half, row, slot].astype(F32)
                for chain in ARRIVE[half]:
                    hops = CHAINS[chain][2]
                    az_copy(chain, hops - 1, part_at)[1].wait_recv()
                    summed = summed + az_buf[chain, hops - 1, part_at].astype(F32)
                a_sum[row, half] = summed.astype(BF16)
            if rows[part_at]:
                ax_copy(rows[part_at]).start()

        when(holder(z), act)
        if rows[part_at]:
            send.started.append((holder(z), ax_copy(rows[part_at])))

    def pieces(distance):
        if distance == 0:
            return [(None, holder(z), half, slot) for half in range(NY)]
        found = []
        for chain in ORDER:
            way, half, hops, _ = CHAINS[chain]
            if distance <= hops:
                goal = turn(z, way * distance, NZ)
                found.append((chain, holder(goal), half, index(goal)))
        return found

    def outward(half):
        return 1 if half == 0 else -1

    def far_copy(half, at):
        way = outward(half)
        return send.build(
            b_in.at[half, turn(x, 2, NX), at], far_buf.at[half, at], far_send.at[half, at],
            far_recv.at[half, at], "context", rank_of(y, turn(x, way, NX), z),
        )

    def near_copy(half, at, way):
        side = 0 if way > 0 else 1
        goal = turn(x, way, NX)
        source = far_buf.at[half, at] if way == outward(half) else b_in.at[half, goal, at]
        return send.build(
            source, near_buf.at[half, at, side], near_send.at[half, at, side],
            near_recv.at[half, at, side], "context", rank_of(y, goal, z),
        )

    def b_start(distance):
        for _, condition, half, at in pieces(distance):
            copies = [far_copy(half, at), near_copy(half, at, -outward(half))]

            def act():
                for copy in copies:
                    copy.start()

            when(condition, act)
            send.started += [(condition, copy) for copy in copies]

    def b_middle(distance):
        for _, condition, half, at in pieces(distance):
            copy = near_copy(half, at, outward(half))

            def act():
                far_copy(half, at).wait_recv()
                add_into(far_buf.at[half, at], b_in.at[half, turn(x, outward(half), NX), at])
                copy.start()

            when(condition, act)
            send.started.append((condition, copy))

    def bz_copy(chain, hop):
        way, half, hops, _ = CHAINS[chain]
        own = b_sum.at[half, index(turn(z, way * (hops - hop), NZ))]
        return send.build(
            own, bz_buf.at[chain, hop], bz_send.at[chain, hop], bz_recv.at[chain, hop],
            "context", rank_of(y, x, turn(z, way, NZ)),
        )

    def b_end(distance):
        for chain, condition, half, at in pieces(distance):
            if chain is not None:
                hop = CHAINS[chain][2] - distance

            def act():
                summed = b_in[half, x, at].astype(F32)
                for way in (1, -1):
                    near_copy(half, at, way).wait_recv()
                    summed = summed + near_buf[half, at, 0 if way > 0 else 1].astype(F32)
                if chain is None:
                    arrivals = [(c, CHAINS[c][2] - 1) for c in ARRIVE[half]]
                else:
                    arrivals = [(chain, hop - 1)] if hop else []
                for other, at_hop in arrivals:
                    bz_copy(other, at_hop).wait_recv()
                    summed = summed + bz_buf[other, at_hop].astype(F32)
                if chain is None:
                    low[1, half] = summed.astype(BF16)
                else:
                    b_sum[half, at] = summed.astype(BF16)
                    bz_copy(chain, hop).start()

            when(condition, act)
            if chain is not None:
                send.started.append((condition, bz_copy(chain, hop)))

    partner = rank_of(1 - y, x, z)
    pairs = [
        send.build(
            low.at[i, 1 - y], y_buf.at[i], y_send.at[i], y_recv.at[i], "context", partner
        )
        for i in range(2)
    ]

    def hand_over(i):
        when(holder(z), pairs[i].start)
        send.started.append((holder(z), pairs[i]))

    def close(i, out):
        def keep():
            out[...] = low[i, y].astype(F32)

        def take():
            pairs[i].wait_recv()
            out[...] = y_buf[i].astype(F32)

        if parity:
            pl.when(holder(z))(keep)
            pl.when(jnp.logical_not(holder(z)))(take)
        else:
            pairs[i].wait_recv()
            out[...] = low[i, y].astype(F32) + y_buf[i].astype(F32)

    def a_row():
        for step in (1, 2, 3):
            ax_copy(step).wait_recv()
        summed = a_sum[x].astype(F32)
        for step in range(3):
            summed = summed + ax_buf[step].astype(F32)
        low[0] = summed.astype(BF16)

    b_start(4)
    b_start(3)
    az(0, 0)
    az(0, 1)
    b_start(2)
    az(0, 2)
    b_start(1)
    az(0, 3)
    b_start(0)
    yield
    b_middle(4)
    b_middle(3)
    az(1, 0)
    az(1, 1)
    b_middle(2)
    b_end(4)
    b_end(3)
    yield
    az(1, 2)
    az(2, 0)
    b_middle(1)
    az(1, 3)
    az(2, 1)
    b_middle(0)
    b_end(2)
    az(3, 0)
    az(2, 2)
    az(3, 1)
    b_end(1)
    a_end(0)
    yield
    az(2, 3)
    az(3, 2)
    a_end(1)
    az(3, 3)
    a_end(2)
    b_end(0)
    hand_over(1)
    a_end(3)
    when(holder(z), a_row)
    hand_over(0)
    close(1, b_out)
    close(0, a_out)
    yield


def block_kernel(
    x_hbm, first_ref, wq_hbm, wk_hbm, wv_hbm, wo_hbm, g_hbm, table_ref,
    attn_ref, gin_ref, gfirst_ref, gwk_ref, gwv_ref,
    x_buf, wq, wkv, wo, g_all, xt, k_own, v_own, k_all, v_all, q_all, cot_all, weights,
    o_acc, dq_acc, o_send, o_recv, dq_send, dq_recv, stat_mine, stat_pair, dk_all, dv_all,
    k_sum, v_sum, part_out, recv_out, part_in, recv_in, acc_in, xt_far,
    pre_own, pre_far, w_part, w_far, w_low, w_last, grad_bufs, local_sem, gather_sems, grad_sems,
    row_send, row_recv, ring_send, ring_recv,
    pair_send, pair_recv, g_send, g_recv, out_send, out_recv, in_send, in_recv,
):
    rank = lax.axis_index("context")
    y, x, z = rank // (NX * NZ), (rank // NZ) % NX, rank % NZ
    tensor, tensors = lax.axis_index("tensor"), lax.axis_size("tensor")
    length, width = x_buf.shape
    columns = q_all.shape[1]
    heads = columns // length
    share = length // tensors
    tile = NH * length
    scale = HD ** (-0.5)
    factor = scale * LOG2E

    def holder(at):
        return lax.rem(at + y, 2) == 0

    place = (y, x, z, holder)
    other = rank_of(1 - y, NX - 1 - x, z)
    peers = [lax.rem(tensor + step, tensors) for step in range(1, tensors)]
    my_rows = pl.ds(pl.multiple_of(tensor * share, share), share)

    loads = [
        pltpu.make_async_copy(source, target, local_sem.at[i])
        for i, (source, target) in enumerate(
            ((x_hbm, x_buf), (wk_hbm, wkv.at[:, :HD]), (wv_hbm, wkv.at[:, HD:]), (g_hbm, g_all.at[my_rows]), (wq_hbm, wq),
             (wo_hbm, wo))
        )
    ]
    for copy in loads:
        copy.start()
    barrier = pltpu.get_barrier_semaphore()
    ranks = [rank_of(1 - y, x, z), rank_of(y, x, turn(z, 1, NZ)), rank_of(y, x, turn(z, -1, NZ))]
    ranks += [rank_of(y, turn(x, step, NX), z) for step in (1, 2, 3)]
    ranks += [rank_of(y, x, turn(z, step, NZ)) for step in range(2, NZ - 1)]
    ranks += [other]
    for who in [{"context": at} for at in ranks] + [{"tensor": at} for at in peers]:
        pl.semaphore_signal(barrier, inc=1, device_id=who, device_id_type=pl.DeviceIdType.MESH)

    cosines, sines = table_ref[:length], table_ref[length : 2 * length]
    mix_here = table_ref[2 * length : 2 * length + 1]
    mix_first = table_ref[2 * length + 1 : 2 * length + 2]

    def spread(table):
        return jnp.concatenate([table] * heads, axis=0)

    def swap(field):
        return jnp.concatenate([field[:, HD // 2 :], field[:, : HD // 2]], axis=1)

    def rot(field, cosine_part, sine_part):
        return field * cosine_part + swap(field) * sine_part

    def stack(field):
        return jnp.concatenate([field[:, h * HD : (h + 1) * HD] for h in range(heads)], axis=0)

    def unstack(field):
        return jnp.concatenate(
            [field[h * length : (h + 1) * length] for h in range(heads)], axis=1
        )

    for copy in loads[:3]:
        copy.wait()
    projected = matmul(x_buf[...], wkv[...], 1, 0)
    k_own[...] = rot(projected[:, :HD], cosines, sines).astype(BF16)
    v_own[...] = (
        mix_here * projected[:, HD:] + mix_first * first_ref[...].astype(F32)
    ).astype(BF16)
    pl.semaphore_wait(barrier, len(ranks) + len(peers))

    send = Sender()
    gather = gather_steps(send, place, k_own, v_own, k_all, v_all, gather_sems)
    next(gather)
    loads[3].wait()
    g_copies = [
        send.go(
            send.build(
                g_all.at[my_rows], g_all.at[my_rows], g_send.at[i], g_recv.at[i], "tensor", peer
            )
        )
        for i, peer in enumerate(peers)
    ]
    loads[4].wait()
    q_all[y] = rot(
        stack(matmul(x_buf[...], wq[...], 1, 0)), spread(cosines), spread(sines)
    ).astype(BF16)
    pair_q = send.go(
        send.build(q_all.at[y], q_all.at[y], pair_send.at[0], pair_recv.at[0], "context", other)
    )
    for _ in range(3):
        next(gather)
    for copy in g_copies:
        copy.wait_recv()
    loads[5].wait()
    for h in range(heads):
        cot_all[y, :, h * length : (h + 1) * length] = matmul(
            wo[h * HD : (h + 1) * HD, :], g_all[...], 1, 1
        ).astype(BF16)
    pair_cot = send.go(
        send.build(cot_all.at[y], cot_all.at[y], pair_send.at[1], pair_recv.at[1], "context", other)
    )
    xt[...] = x_buf[...].T.reshape(xt.shape)
    next(gather)
    row_x = []
    for step in (1, 3, 2):
        goal = turn(x, step, NX)
        row_x.append(
            send.go(
                send.build(
                    xt.at[:, goal], xt_far.at[step - 1], row_send.at[step - 1],
                    row_recv.at[step - 1], "context", rank_of(y, goal, z),
                )
            )
        )
    pair_q.wait_recv()

    key_in_tile = lax.broadcasted_iota(jnp.int32, (tile, columns), 0)
    key_in_tile = (2 * (key_in_tile // length) + y) * length + lax.rem(key_in_tile, length)
    query_in_block = lax.rem(lax.broadcasted_iota(jnp.int32, (tile, columns), 1), length)
    def row_of(slot):
        return jnp.where(slot == y, y * NX + x, slot * NX + NX - 1 - x)

    def tile_of(ref, row):
        return ref[row // NX, lax.rem(row, NX)].reshape(tile, HD)

    @pl.loop(0, 2)
    def _(slot):
        last = row_of(slot)
        visible = key_in_tile <= query_in_block + z * length
        queries = q_all[slot].astype(F32).T.astype(BF16)

        def scores(row):
            return matmul(tile_of(k_all, row), queries, 1, 0)

        def max_step(row, current):
            return jnp.maximum(current, jnp.max(scores(row), axis=0, keepdims=True))

        top = jnp.max(jnp.where(visible, scores(last), NEGATIVE), axis=0, keepdims=True)
        top = lax.fori_loop(0, last, max_step, top) * factor

        def weigh(row, current, masked):
            totals, output = current
            exponent = scores(row) * factor - top
            if masked:
                exponent = jnp.where(visible, exponent, NEGATIVE)
            weight = jnp.exp2(exponent)
            totals = totals + jnp.sum(weight, axis=0, keepdims=True)
            low = weight.astype(BF16)
            weights[slot * NX + row] = low
            return totals, output + matmul(tile_of(v_all, row), low, 0, 0)

        start = (jnp.zeros((1, columns), F32), jnp.zeros((HD, columns), F32))
        start = weigh(last, start, True)
        totals, output = lax.fori_loop(
            0, last, lambda row, current: weigh(row, current, False), start
        )
        stat_mine[slot, 0:1] = top
        stat_mine[slot, 1:2] = totals
        o_acc[slot] = output

    pair_cot.wait_recv()
    for slot in range(2):
        stat_mine[slot, 2:3] = jnp.sum(
            cot_all[slot].astype(F32) * o_acc[slot], axis=0, keepdims=True
        )
    pair_stat = send.go(
        send.build(stat_mine, stat_pair, pair_send.at[2], pair_recv.at[2], "context", other)
    )
    o_send[...] = o_acc[1 - y].astype(BF16)
    pair_o = send.go(
        send.build(o_send, o_recv, pair_send.at[3], pair_recv.at[3], "context", other)
    )
    dk_all[...] = jnp.zeros(dk_all.shape, BF16)
    dv_all[...] = jnp.zeros(dv_all.shape, BF16)
    pair_stat.wait_recv()

    def merged(slot):
        top = jnp.maximum(stat_mine[slot, 0:1], stat_pair[slot, 0:1])
        mine = jnp.exp2(stat_mine[slot, 0:1] - top)
        theirs = jnp.exp2(stat_pair[slot, 0:1] - top)
        inverse = 1.0 / (stat_mine[slot, 1:2] * mine + stat_pair[slot, 1:2] * theirs)
        return mine * inverse, theirs * inverse

    @pl.loop(0, 2)
    def _(step):
        slot = 1 - step
        mine, theirs = merged(slot)
        delta = (stat_mine[slot, 2:3] * mine + stat_pair[slot, 2:3] * theirs) * mine
        scaled = cot_all[slot].astype(F32) * mine
        scaled_across = scaled.astype(BF16)
        scaled_rows = scaled.T.astype(BF16)
        queries = q_all[slot]

        def back(row, query_grad):
            low = weights[slot * NX + row]
            change = matmul(tile_of(v_all, row), scaled_across, 1, 0) - delta
            score_grad = (low.astype(F32) * change).astype(BF16)
            key_term = matmul(score_grad, queries, 1, 0) * scale
            value_term = matmul(low, scaled_rows, 1, 0)
            shape = (NH, length, HD)
            at = (row // NX, lax.rem(row, NX))
            dk_all[at] = (dk_all[at].astype(F32) + key_term.reshape(shape)).astype(BF16)
            dv_all[at] = (dv_all[at].astype(F32) + value_term.reshape(shape)).astype(BF16)
            return query_grad + matmul(tile_of(k_all, row), score_grad, 0, 0)

        dq_acc[slot] = lax.fori_loop(
            0, row_of(slot) + 1, back, jnp.zeros((HD, columns), F32)
        )

    scatter = fold_steps(
        send, place, True, dk_all, dv_all, k_sum, v_sum, grad_bufs, grad_sems
    )
    next(scatter)
    dq_send[...] = dq_acc[1 - y].astype(BF16)
    pair_dq = send.go(
        send.build(dq_send, dq_recv, pair_send.at[4], pair_recv.at[4], "context", other)
    )

    def share_out(part, recv, send_sem, recv_sem):
        return [
            send.go(
                send.build(
                    part.at[peer], recv.at[i], send_sem.at[i], recv_sem.at[i], "tensor", peer
                )
            )
            for i, peer in enumerate(peers)
        ]

    def add_up(part, recv, copies, out):
        for copy in copies:
            copy.wait_recv()
        summed = part[tensor].astype(F32)
        for i in range(len(copies)):
            summed = summed + recv[i].astype(F32)
        out[...] = summed.astype(BF16)

    strip = min(512, width)

    def strip_of(index):
        return pl.ds(pl.multiple_of(index * strip, strip), strip)

    pair_o.wait_recv()
    mine, theirs = merged(y)
    outputs = unstack(
        (o_acc[y] * mine + o_recv[...].astype(F32) * theirs).T.astype(BF16)
    )

    @pl.loop(0, width // strip)
    def _(index):
        at = strip_of(index)
        term = matmul(outputs, wo[:, at], 1, 0).astype(BF16)
        for peer in range(tensors):
            part_out[peer, :, at] = term[peer * share : (peer + 1) * share]

    out_copies = share_out(part_out, recv_out, out_send, out_recv)
    next(scatter)
    pair_dq.wait_recv()
    query_pre = unstack(
        rot(
            (dq_acc[y] + dq_recv[...].astype(F32)).T * scale, spread(cosines), -spread(sines)
        ).astype(BF16)
    )

    @pl.loop(0, width // strip)
    def _(index):
        at = strip_of(index)
        acc_in[:, at] = matmul(query_pre, wq[at, :], 1, 1)

    next(scatter)
    add_up(part_out, recv_out, out_copies, attn_ref)
    next(scatter)
    key_pre = rot(k_sum[...], cosines, -sines).astype(BF16)
    value_sum = v_sum[...]
    value_pre = (mix_here * value_sum).astype(BF16)
    pre_own[...] = jnp.concatenate([key_pre, value_pre], axis=1)
    row_pre = []
    for step in (2, 1, 3):
        row_pre.append(
            send.go(
                send.build(
                    pre_own, pre_far.at[step - 1], row_send.at[2 + step], row_recv.at[2 + step],
                    "context", rank_of(y, turn(x, step, NX), z),
                )
            )
        )
    gfirst_ref[...] = (mix_first * value_sum).astype(BF16)

    @pl.loop(0, width // strip)
    def _(index):
        at = strip_of(index)
        term = (acc_in[:, at] + matmul(pre_own[...], wkv[at, :], 1, 1)).astype(BF16)
        for peer in range(tensors):
            part_in[peer, :, at] = term[peer * share : (peer + 1) * share]

    in_copies = share_out(part_in, recv_in, in_send, in_recv)
    many, rows = w_part.shape[1], w_part.shape[2]

    def term_of(side, pre):
        return matmul(side.reshape(NY * many * rows, length), pre, 1, 0)

    for copy in row_x + row_pre:
        copy.wait_recv()
    summed = term_of(xt[:, x], pre_own[...])
    for i in range(NX - 1):
        summed = summed + term_of(xt_far[i], pre_far[i])
    w_part[...] = summed.astype(BF16).reshape(w_part.shape)
    ring = []
    for step in (4, 3, 5, 2, 6, 1, 7):
        goal = turn(z, step, NZ)
        ring.append(
            send.go(
                send.build(
                    w_part.at[:, goal], w_far.at[step - 1], ring_send.at[step - 1],
                    ring_recv.at[step - 1], "context", rank_of(y, x, goal),
                )
            )
        )
    add_up(part_in, recv_in, in_copies, gin_ref)
    for copy in ring:
        copy.wait_recv()

    def strip_sum(half):
        total = w_part[half, z].astype(F32)
        for i in range(NZ - 1):
            total = total + w_far[i, half].astype(F32)
        return total

    w_low[...] = strip_sum(1 - y).astype(BF16)
    pair_w = send.go(
        send.build(
            w_low, w_last, pair_send.at[5], pair_recv.at[5], "context", rank_of(1 - y, x, z)
        )
    )
    weight = strip_sum(y)
    pair_w.wait_recv()
    weight = weight + w_last[...].astype(F32)
    gwk_ref[...] = weight[:, :HD]
    gwv_ref[...] = weight[:, HD:]
    send.finish()


def store_kernel(*refs):
    count = len(refs) // 2
    for i in range(count):
        refs[count + i][...] = refs[i][...]


def rope_tables(positions, head_width):
    half_width = head_width // 2
    exponent = jnp.arange(half_width, dtype=F32) * (2.0 / head_width)
    frequency = jnp.power(jnp.float32(THETA), -exponent)
    angles = positions.astype(F32)[:, None] * frequency[None, :]
    return (jnp.cos(angles), jnp.sin(angles))


def shards(hidden_in, value_first, w_query, w_key, w_value, w_out, value_mix, grad_out):
    tensors = lax.axis_size("tensor")
    length, width = hidden_in.shape[1:]
    features = w_query.shape[1]
    columns = features // HD * length
    share = length // tensors
    rows = width // (NY * NX * NZ)
    block_rows = lax.axis_index("context") * length + jnp.arange(length, dtype=jnp.int32)
    cosines, sines = rope_tables(block_rows, HD)
    tables = jnp.concatenate(
        [
            jnp.concatenate([cosines, cosines], axis=1),
            jnp.concatenate([-sines, sines], axis=1),
            jnp.broadcast_to(value_mix[:, :1], (2, HD)),
            jnp.zeros((6, HD), F32),
        ],
        axis=0,
    )
    vmem = pl.BlockSpec(memory_space=pltpu.VMEM)
    hbm = pl.BlockSpec(memory_space=pl.ANY)
    dma = pltpu.SemaphoreType.DMA

    def low(*shape):
        return pltpu.VMEM(shape, BF16)

    def full(*shape):
        return pltpu.VMEM(shape, F32)

    def fold_room(ends, count):
        return (
            low(4, 4, NX, count, HD), low(NY, ends, count, HD), low(NY, ends, 2, count, HD),
            low(4, 4, count, HD), low(NX, NY, count, HD), low(NY, ends, count, HD),
            low(3, NY, count, HD), low(2, NY, count, HD), low(2, count, HD),
        )

    others = (max(tensors - 1, 1),)
    scratch = [
        low(length, width), low(width, features), low(width, 2 * HD),
        low(features, width), low(length, width), low(NY, NX, NZ * rows, length), low(length, HD),
        low(length, HD), low(NY, NX, NH, length, HD), low(NY, NX, NH, length, HD),
        low(2, columns, HD), low(2, HD, columns), low(3 * NX, NH * length, columns),
        full(2, HD, columns), full(2, HD, columns), low(HD, columns), low(HD, columns),
        low(HD, columns), low(HD, columns), full(2, 8, columns), full(2, 8, columns),
        low(NY, NX, NH, length, HD), low(NY, NX, NH, length, HD), full(length, HD),
        full(length, HD), low(tensors, share, width), low(others[0], share, width),
        low(tensors, share, width), low(others[0], share, width), full(length, width),
        low(NX - 1, NY, NZ * rows, length), low(length, 2 * HD), low(NX - 1, length, 2 * HD),
        low(NY, NZ, rows, 2 * HD), low(NZ - 1, NY, rows, 2 * HD), low(rows, 2 * HD),
        low(rows, 2 * HD),
        fold_room(NH, length), dma((6,)),
        (dma((2,)), dma((2,)), dma((3,)), dma((3,)), dma((4, 4)), dma((4, 4)), dma((4, 4, NX)),
         dma((4, 4, NX)), dma((NY, NH, 2)), dma((NY, NH, 2)), dma((NY, NH)), dma((NY, NH))),
    ]

    def fold_sems(ends):
        return (
            dma((4, 4, NX)), dma((4, 4, NX)), dma((NY, ends)), dma((NY, ends)),
            dma((NY, ends, 2)), dma((NY, ends, 2)), dma((4, 4)), dma((4, 4)), dma((3,)), dma((3,)),
            dma((2,)), dma((2,)),
        )

    scratch += [fold_sems(NH), dma((6,)), dma((6,)), dma((NZ - 1,)), dma((NZ - 1,))]
    scratch += [dma((6,)), dma((6,))] + [dma(others)] * 6
    results = pl.pallas_call(
        block_kernel,
        out_shape=(
            jax.ShapeDtypeStruct((share, width), BF16),
            jax.ShapeDtypeStruct((share, width), BF16),
            jax.ShapeDtypeStruct((length, HD), BF16),
            jax.ShapeDtypeStruct((rows, HD), F32),
            jax.ShapeDtypeStruct((rows, HD), F32),
        ),
        in_specs=[hbm, vmem, hbm, hbm, hbm, hbm, hbm, vmem],
        out_specs=(vmem,) * 5,
        scratch_shapes=scratch,
        compiler_params=pltpu.CompilerParams(
            collective_id=1, has_side_effects=True, vmem_limit_bytes=56 * 2**20
        ),
        name="attention_block",
    )(
        hidden_in.reshape(length, width), value_first.reshape(length, HD), w_query, w_key, w_value,
        w_out, grad_out.reshape(share, width), tables,
    )
    attn_out, grad_in, grad_first, key_weight, value_weight = pl.pallas_call(
        store_kernel,
        out_shape=tuple(jax.ShapeDtypeStruct(part.shape, part.dtype) for part in results),
        in_specs=[vmem] * len(results),
        out_specs=(vmem,) * len(results),
        name="store_results",
    )(*results)
    return (
        attn_out.reshape(1, share, width),
        grad_in.reshape(1, share, width),
        grad_first.reshape(1, length, HD),
        key_weight,
        value_weight,
    )


def solution(mesh):
    return jax.shard_map(
        shards,
        mesh=mesh,
        in_specs=(
            P("context", None, None),
            P("context", None, "tensor"),
            P(None, "tensor"),
            P(None, "tensor"),
            P(None, "tensor"),
            P("tensor", None),
            P(None, "tensor"),
            P("context", "tensor", None),
        ),
        out_specs=(
            P("context", "tensor", None),
            P("context", "tensor", None),
            P("context", None, "tensor"),
            P("context", "tensor"),
            P("context", "tensor"),
        ),
        check_vma=False,
    )
```

```python
import jax
import jax.numpy as jnp
from jax import lax
from jax.experimental import pallas as pl
from jax.experimental.pallas import tpu as pltpu
from jax.sharding import PartitionSpec as P

HD = 128
THETA = 500000.0
LOG2E = 1.4426950408889634
NEGATIVE = -1e30
NY, NX, NZ = 2, 4, 8
NH = NZ // 2
F32, BF16 = jnp.float32, jnp.bfloat16

CHAINS = ((1, 0, 4, 2), (1, 1, 3, 1), (-1, 1, 4, 2), (-1, 0, 3, 1))
ORDER = (0, 2, 1, 3)
ARRIVE = ((0, 3), (1, 2))


def rank_of(y, x, z):
    return (y * NX + x) * NZ + z


def turn(value, step, count):
    return lax.rem(value + (step + count), count)


def when(condition, action):
    if condition is True:
        action()
    else:
        pl.when(condition)(action)


def matmul(left, right, left_dim, right_dim):
    return lax.dot_general(
        left, right, (((left_dim,), (right_dim,)), ((), ())), preferred_element_type=F32
    )


def add_into(target, term):
    target[...] = (target[...].astype(F32) + term[...].astype(F32)).astype(BF16)


class Sender:
    def __init__(self):
        self.started = []

    def build(self, source, target, send_sem, recv_sem, axis, rank):
        return pltpu.make_async_remote_copy(
            src_ref=source,
            dst_ref=target,
            send_sem=send_sem,
            recv_sem=recv_sem,
            device_id={axis: rank},
            device_id_type=pl.DeviceIdType.MESH,
        )

    def go(self, copy, condition=True):
        copy.start()
        self.started.append((condition, copy))
        return copy

    def finish(self):
        for condition, copy in self.started:
            when(condition, copy.wait_send)


class Place:
    def __init__(self):
        rank = lax.axis_index("context")
        self.rank = rank
        self.y, self.x, self.z = rank // (NX * NZ), (rank // NZ) % NX, rank % NZ
        self.z_ring = [lax.rem(self.z + step, NZ) for step in range(NZ)]
        self.x_ring = [lax.rem(self.x + step, NX) for step in range(NX)]
        self.halves = [at // 2 for at in self.z_ring]
        even = lax.rem(self.z + self.y, 2) == 0
        self.parity = (even, jnp.logical_not(even))

    def z_at(self, step):
        return self.z_ring[step % NZ]

    def x_at(self, step):
        return self.x_ring[step % NX]

    def half(self, step):
        return self.halves[step % NZ]

    def holds(self, step):
        return self.parity[step % 2]


def gather_steps(send, place, k_own, v_own, k_all, v_all, sems):
    y, x, z = place.y, place.x, place.z
    y_send, y_recv, kx_send, kx_recv, vz_send, vz_recv, kz_send, kz_recv = sems[:8]
    vx_send, vx_recv, vf_send, vf_recv = sems[8:]
    slot = place.half(0)
    partner = rank_of(1 - y, x, z)
    lends = place.holds(1)
    pairs = [
        send.build(own, whole.at[y, x, slot], y_send.at[i], y_recv.at[i], "context", partner)
        for i, (own, whole) in enumerate(((k_own, k_all), (v_own, v_all)))
    ]

    def lend():
        for copy in pairs:
            copy.start()

    def keep():
        k_all[y, x, slot] = k_own[...]
        v_all[y, x, slot] = v_own[...]

    pl.when(lends)(lend)
    pl.when(place.holds(0))(keep)
    send.started += [(lends, copy) for copy in pairs]

    kx = {}
    for step in (1, 3, 2):
        part = k_all.at[:, x, slot]
        kx[step] = send.build(
            part, part, kx_send.at[step - 1], kx_recv.at[step - 1], "context",
            rank_of(y, place.x_at(step), z),
        )
    rows = (0, 1, 3, 2)

    def kz_copy(chain, hop, part_at):
        way, half, _, _ = CHAINS[chain]
        part = k_all.at[half, place.x_at(rows[part_at]), place.half(-way * hop)]
        return send.build(
            part, part, kz_send.at[chain, hop, part_at], kz_recv.at[chain, hop, part_at],
            "context", rank_of(y, x, place.z_at(way)),
        )

    def kz(hop, part_at):
        if hop == 0 and part_at:
            pl.when(place.holds(0))(kx[NX - rows[part_at]].wait_recv)
        for chain in ORDER:
            if hop < CHAINS[chain][2]:
                condition = place.holds(-CHAINS[chain][0] * hop)
                copy = kz_copy(chain, hop, part_at)

                def act():
                    if hop:
                        kz_copy(chain, hop - 1, part_at).wait_recv()
                    copy.start()

                when(condition, act)
                send.started.append((condition, copy))

    def vz_copy(chain, hop):
        way, half, _, _ = CHAINS[chain]
        part = v_all.at[half, x, place.half(-way * hop)]
        return send.build(
            part, part, vz_send.at[chain, hop], vz_recv.at[chain, hop], "context",
            rank_of(y, x, place.z_at(way)),
        )

    def vx_copy(half, at, way):
        part = v_all.at[half, x, at]
        side = 0 if way > 0 else 1
        return send.build(
            part, part, vx_send.at[half, at, side], vx_recv.at[half, at, side], "context",
            rank_of(y, place.x_at(way), z),
        )

    def vf_copy(half, at):
        way = 1 if half == 0 else -1
        part = v_all.at[half, place.x_at(-way), at]
        return send.build(
            part, part, vf_send.at[half, at], vf_recv.at[half, at], "context",
            rank_of(y, place.x_at(way), z),
        )

    def pieces(distance):
        if distance == 0:
            return [(None, place.holds(0), half, slot) for half in range(NY)]
        found = []
        for chain in ORDER:
            way, half, hops, _ = CHAINS[chain]
            if distance <= hops:
                step = -way * distance
                found.append((chain, place.holds(step), half, place.half(step)))
        return found

    def v_round(distance):
        for chain, condition, half, at in pieces(distance):
            copies = [vx_copy(half, at, 1), vx_copy(half, at, -1)]
            if chain is None:
                copies += [vz_copy(c, 0) for c in ORDER if CHAINS[c][1] == half]
            elif distance < CHAINS[chain][2]:
                copies.insert(0, vz_copy(chain, distance))

            def act():
                if chain is not None:
                    vz_copy(chain, distance - 1).wait_recv()
                for copy in copies:
                    copy.start()

            when(condition, act)
            send.started += [(condition, copy) for copy in copies]

    def forward(distance):
        for _, condition, half, at in pieces(distance):
            copy = vf_copy(half, at)

            def act():
                vx_copy(half, at, 1 if half == 0 else -1).wait_recv()
                copy.start()

            when(condition, act)
            send.started.append((condition, copy))

    def finish():
        for distance in range(5):
            for _, condition, half, at in pieces(distance):

                def act():
                    vx_copy(half, at, -1 if half == 0 else 1).wait_recv()
                    vf_copy(half, at).wait_recv()

                when(condition, act)
        for chain in ORDER:
            way, _, hops, _ = CHAINS[chain]
            condition = place.holds(-way * hops)

            def act():
                for part_at in range(NX):
                    kz_copy(chain, hops - 1, part_at).wait_recv()

            when(condition, act)

    yield

    def start_rows():
        for copy in pairs:
            copy.wait_recv()
        for copy in kx.values():
            copy.start()

    pl.when(place.holds(0))(start_rows)
    send.started += [(place.holds(0), copy) for copy in kx.values()]
    v_round(0)
    kz(0, 0)
    v_round(1)
    kz(0, 1)
    kz(1, 0)
    forward(0)
    yield
    v_round(2)
    kz(0, 2)
    kz(1, 1)
    kz(2, 0)
    forward(1)
    yield
    v_round(3)
    kz(0, 3)
    kz(1, 2)
    kz(2, 1)
    kz(3, 0)
    forward(2)
    v_round(4)
    kz(1, 3)
    kz(2, 2)
    kz(3, 1)
    forward(3)
    kz(2, 3)
    kz(3, 2)
    forward(4)
    kz(3, 3)
    yield
    finish()
    yield


def fold_steps(send, place, idle, a_in, b_in, a_out, b_out, bufs, sems):
    y, x, z = place.y, place.x, place.z

    az_buf, far_buf, near_buf, bz_buf, a_sum, b_sum, ax_buf, low, y_buf = bufs
    az_send, az_recv, far_send, far_recv, near_send, near_recv, bz_send, bz_recv = sems[:8]
    ax_send, ax_recv, y_send, y_recv = sems[8:]
    slot = place.half(0)
    rows = (2, 1, 3, 0)

    def az_copy(chain, hop, part_at):
        way, half, hops, _ = CHAINS[chain]
        own = a_in.at[half, place.x_at(rows[part_at]), place.half(way * (hops - hop))]
        source = az_buf.at[chain, hop - 1, part_at] if hop else own
        copy = send.build(
            source, az_buf.at[chain, hop, part_at], az_send.at[chain, hop, part_at],
            az_recv.at[chain, hop, part_at], "context", rank_of(y, x, place.z_at(way)),
        )
        return own, copy

    def az(hop, part_at):
        for chain in ORDER:
            way, _, hops, _ = CHAINS[chain]
            if hop < hops:
                condition = place.holds(way * (hops - hop))
                own, copy = az_copy(chain, hop, part_at)

                def act():
                    if hop:
                        az_copy(chain, hop - 1, part_at)[1].wait_recv()
                        add_into(az_buf.at[chain, hop - 1, part_at], own)
                    copy.start()

                when(condition, act)
                send.started.append((condition, copy))

    def ax_copy(step):
        goal = place.x_at(step)
        return send.build(
            a_sum.at[goal], ax_buf.at[step - 1], ax_send.at[step - 1], ax_recv.at[step - 1],
            "context", rank_of(y, goal, z),
        )

    def a_end(part_at):
        row = place.x_at(rows[part_at])

        def act():
            for half in range(NY):
                summed = a_in[half, row, slot].astype(F32)
                for chain in ARRIVE[half]:
                    hops = CHAINS[chain][2]
                    az_copy(chain, hops - 1, part_at)[1].wait_recv()
                    summed = summed + az_buf[chain, hops - 1, part_at].astype(F32)
                a_sum[row, half] = summed.astype(BF16)
            if rows[part_at]:
                ax_copy(rows[part_at]).start()

        when(place.holds(0), act)
        if rows[part_at]:
            send.started.append((place.holds(0), ax_copy(rows[part_at])))

    def pieces(distance):
        if distance == 0:
            return [(None, place.holds(0), half, slot) for half in range(NY)]
        found = []
        for chain in ORDER:
            way, half, hops, _ = CHAINS[chain]
            if distance <= hops:
                step = way * distance
                found.append((chain, place.holds(step), half, place.half(step)))
        return found

    def outward(half):
        return 1 if half == 0 else -1

    def far_copy(half, at):
        way = outward(half)
        return send.build(
            b_in.at[half, place.x_at(2), at], far_buf.at[half, at], far_send.at[half, at],
            far_recv.at[half, at], "context", rank_of(y, place.x_at(way), z),
        )

    def near_copy(half, at, way):
        side = 0 if way > 0 else 1
        goal = place.x_at(way)
        source = far_buf.at[half, at] if way == outward(half) else b_in.at[half, goal, at]
        return send.build(
            source, near_buf.at[half, at, side], near_send.at[half, at, side],
            near_recv.at[half, at, side], "context", rank_of(y, goal, z),
        )

    def b_start(distance):
        for _, condition, half, at in pieces(distance):
            copies = [far_copy(half, at), near_copy(half, at, -outward(half))]

            def act():
                for copy in copies:
                    copy.start()

            when(condition, act)
            send.started += [(condition, copy) for copy in copies]

    def b_middle(distance):
        for _, condition, half, at in pieces(distance):
            copy = near_copy(half, at, outward(half))

            def act():
                far_copy(half, at).wait_recv()
                add_into(far_buf.at[half, at], b_in.at[half, place.x_at(outward(half)), at])
                copy.start()

            when(condition, act)
            send.started.append((condition, copy))

    def bz_copy(chain, hop):
        way, half, hops, _ = CHAINS[chain]
        own = b_sum.at[half, place.half(way * (hops - hop))]
        return send.build(
            own, bz_buf.at[chain, hop], bz_send.at[chain, hop], bz_recv.at[chain, hop],
            "context", rank_of(y, x, place.z_at(way)),
        )

    def b_end(distance):
        for chain, condition, half, at in pieces(distance):
            if chain is not None:
                hop = CHAINS[chain][2] - distance

            def act():
                summed = b_in[half, x, at].astype(F32)
                for way in (1, -1):
                    near_copy(half, at, way).wait_recv()
                    summed = summed + near_buf[half, at, 0 if way > 0 else 1].astype(F32)
                if chain is None:
                    arrivals = [(c, CHAINS[c][2] - 1) for c in ARRIVE[half]]
                else:
                    arrivals = [(chain, hop - 1)] if hop else []
                for other, at_hop in arrivals:
                    bz_copy(other, at_hop).wait_recv()
                    summed = summed + bz_buf[other, at_hop].astype(F32)
                if chain is None:
                    low[1, half] = summed.astype(BF16)
                else:
                    b_sum[half, at] = summed.astype(BF16)
                    bz_copy(chain, hop).start()

            when(condition, act)
            if chain is not None:
                send.started.append((condition, bz_copy(chain, hop)))

    partner = rank_of(1 - y, x, z)
    pairs = [
        send.build(
            low.at[i, 1 - y], y_buf.at[i], y_send.at[i], y_recv.at[i], "context", partner
        )
        for i in range(2)
    ]

    def hand_over(i):
        when(place.holds(0), pairs[i].start)
        send.started.append((place.holds(0), pairs[i]))

    def close(i, out):
        def keep():
            out[...] = low[i, y].astype(F32)

        def take():
            pairs[i].wait_recv()
            out[...] = y_buf[i].astype(F32)

        pl.when(place.holds(0))(keep)
        pl.when(place.holds(1))(take)

    def a_row():
        for step in (1, 2, 3):
            ax_copy(step).wait_recv()
        summed = a_sum[x].astype(F32)
        for step in range(3):
            summed = summed + ax_buf[step].astype(F32)
        low[0] = summed.astype(BF16)

    b_start(4)
    b_start(3)
    az(0, 0)
    az(0, 1)
    b_start(2)
    az(0, 2)
    b_start(1)
    az(0, 3)
    b_start(0)
    yield
    for work, arguments in (
        (b_middle, (4,)), (b_middle, (3,)), (az, (1, 0)), (az, (1, 1)), (b_middle, (2,)),
        (b_end, (4,)), (b_end, (3,)), (az, (1, 2)), (az, (2, 0)), (b_middle, (1,)), (az, (1, 3)),
        (az, (2, 1)), (b_middle, (0,)), (b_end, (2,)), (az, (3, 0)), (az, (2, 2)), (az, (3, 1)),
        (b_end, (1,)), (a_end, (0,)), (az, (2, 3)), (az, (3, 2)), (a_end, (1,)), (az, (3, 3)),
        (a_end, (2,)), (b_end, (0,)),
    ):
        work(*arguments)
        idle()
    hand_over(1)
    a_end(3)
    when(place.holds(0), a_row)
    hand_over(0)
    close(1, b_out)
    close(0, a_out)
    yield


def block_kernel(
    x_hbm, first_ref, wq_hbm, wk_hbm, wv_hbm, wo_hbm, g_hbm, table_ref,
    attn_ref, gin_ref, gfirst_ref, gwk_ref, gwv_ref,
    x_buf, wq, wkv, wo, g_all, xt, k_own, v_own, k_all, v_all, q_all, cot_all, weights,
    o_acc, dq_acc, o_send, o_recv, dq_send, dq_recv, stat_mine, stat_pair, dk_all, dv_all,
    k_sum, v_sum, part_out, recv_out, part_in, recv_in, xt_far,
    pre_own, pre_far, w_part, w_far, w_low, w_last, grad_bufs, local_sem, gather_sems, grad_sems,
    row_send, row_recv, ring_send, ring_recv,
    pair_send, pair_recv, g_send, g_recv, out_send, out_recv, in_send, in_recv,
):
    place = Place()
    y, x, z = place.y, place.x, place.z
    tensor, tensors = lax.axis_index("tensor"), lax.axis_size("tensor")
    length, width = x_buf.shape
    columns = q_all.shape[1]
    heads = columns // length
    share = length // tensors
    tile = NH * length
    scale = HD ** (-0.5)
    factor = scale * LOG2E

    other = rank_of(1 - y, NX - 1 - x, z)
    peers = [lax.rem(tensor + step, tensors) for step in range(1, tensors)]
    my_rows = pl.ds(pl.multiple_of(tensor * share, share), share)

    loads = [
        pltpu.make_async_copy(source, target, local_sem.at[i])
        for i, (source, target) in enumerate(
            ((x_hbm, x_buf), (wk_hbm, wkv.at[:, :HD]), (wv_hbm, wkv.at[:, HD:]), (g_hbm, g_all.at[my_rows]), (wq_hbm, wq),
             (wo_hbm, wo))
        )
    ]
    for copy in loads:
        copy.start()
    barrier = pltpu.get_barrier_semaphore()
    ranks = [rank_of(1 - y, x, z), rank_of(y, x, turn(z, 1, NZ)), rank_of(y, x, turn(z, -1, NZ))]
    ranks += [rank_of(y, turn(x, step, NX), z) for step in (1, 2, 3)]
    ranks += [rank_of(y, x, turn(z, step, NZ)) for step in range(2, NZ - 1)]
    ranks += [other]
    for who in [{"context": at} for at in ranks] + [{"tensor": at} for at in peers]:
        pl.semaphore_signal(barrier, inc=1, device_id=who, device_id_type=pl.DeviceIdType.MESH)

    cosines, sines = table_ref[:length], table_ref[length : 2 * length]
    mix_here = table_ref[2 * length : 2 * length + 1]
    mix_first = table_ref[2 * length + 1 : 2 * length + 2]

    def spread(table):
        return jnp.concatenate([table] * heads, axis=0)

    def swap(field):
        return jnp.concatenate([field[:, HD // 2 :], field[:, : HD // 2]], axis=1)

    def rot(field, cosine_part, sine_part):
        return field * cosine_part + swap(field) * sine_part

    def stack(field):
        return jnp.concatenate([field[:, h * HD : (h + 1) * HD] for h in range(heads)], axis=0)

    def unstack(field):
        return jnp.concatenate(
            [field[h * length : (h + 1) * length] for h in range(heads)], axis=1
        )

    for copy in loads[:3]:
        copy.wait()
    projected = matmul(x_buf[...], wkv[...], 1, 0)
    k_own[...] = rot(projected[:, :HD], cosines, sines).astype(BF16)
    v_own[...] = (
        mix_here * projected[:, HD:] + mix_first * first_ref[...].astype(F32)
    ).astype(BF16)
    pl.semaphore_wait(barrier, len(ranks) + len(peers))

    send = Sender()
    gather = gather_steps(send, place, k_own, v_own, k_all, v_all, gather_sems)
    next(gather)
    loads[3].wait()
    g_copies = [
        send.go(
            send.build(
                g_all.at[my_rows], g_all.at[my_rows], g_send.at[i], g_recv.at[i], "tensor", peer
            )
        )
        for i, peer in enumerate(peers)
    ]
    loads[4].wait()
    q_all[y] = rot(
        stack(matmul(x_buf[...], wq[...], 1, 0)), spread(cosines), spread(sines)
    ).astype(BF16)
    pair_q = send.go(
        send.build(q_all.at[y], q_all.at[y], pair_send.at[0], pair_recv.at[0], "context", other)
    )
    for _ in range(3):
        next(gather)
    for copy in g_copies:
        copy.wait_recv()
    loads[5].wait()
    cotangent = matmul(wo[...], g_all[...], 1, 1).astype(BF16)
    for h in range(heads):
        cot_all[y, :, h * length : (h + 1) * length] = cotangent[h * HD : (h + 1) * HD]
    pair_cot = send.go(
        send.build(cot_all.at[y], cot_all.at[y], pair_send.at[1], pair_recv.at[1], "context", other)
    )
    xt[...] = x_buf[...].T.reshape(xt.shape)
    next(gather)
    row_x = []
    for step in (1, 3, 2):
        goal = turn(x, step, NX)
        row_x.append(
            send.go(
                send.build(
                    xt.at[:, goal], xt_far.at[step - 1], row_send.at[step - 1],
                    row_recv.at[step - 1], "context", rank_of(y, goal, z),
                )
            )
        )
    pair_q.wait_recv()

    key_in_tile = lax.broadcasted_iota(jnp.int32, (tile, columns), 0)
    key_in_tile = (2 * (key_in_tile // length) + y) * length + lax.rem(key_in_tile, length)
    query_in_block = lax.rem(lax.broadcasted_iota(jnp.int32, (tile, columns), 1), length)
    def row_of(slot):
        return jnp.where(slot == y, y * NX + x, slot * NX + NX - 1 - x)

    def tile_of(ref, row):
        return ref[row // NX, lax.rem(row, NX)].reshape(tile, HD)

    @pl.loop(0, 2)
    def _(slot):
        last = row_of(slot)
        visible = key_in_tile <= query_in_block + z * length
        queries = q_all[slot].astype(F32).T.astype(BF16)

        def scores(row):
            return matmul(tile_of(k_all, row), queries, 1, 0)

        def max_step(row, current):
            return jnp.maximum(current, jnp.max(scores(row), axis=0, keepdims=True))

        top = jnp.max(jnp.where(visible, scores(last), NEGATIVE), axis=0, keepdims=True)
        top = lax.fori_loop(0, last, max_step, top) * factor

        def weigh(row, current, masked):
            totals, output = current
            exponent = scores(row) * factor - top
            if masked:
                exponent = jnp.where(visible, exponent, NEGATIVE)
            weight = jnp.exp2(exponent)
            totals = totals + jnp.sum(weight, axis=0, keepdims=True)
            low = weight.astype(BF16)
            weights[slot * NX + row] = low
            return totals, output + matmul(tile_of(v_all, row), low, 0, 0)

        start = (jnp.zeros((1, columns), F32), jnp.zeros((HD, columns), F32))
        start = weigh(last, start, True)
        totals, output = lax.fori_loop(
            0, last, lambda row, current: weigh(row, current, False), start
        )
        stat_mine[slot, 0:1] = top
        stat_mine[slot, 1:2] = totals
        o_acc[slot] = output

    pair_cot.wait_recv()
    for slot in range(2):
        stat_mine[slot, 2:3] = jnp.sum(
            cot_all[slot].astype(F32) * o_acc[slot], axis=0, keepdims=True
        )
    pair_stat = send.go(
        send.build(stat_mine, stat_pair, pair_send.at[2], pair_recv.at[2], "context", other)
    )
    o_send[...] = o_acc[1 - y].astype(BF16)
    pair_o = send.go(
        send.build(o_send, o_recv, pair_send.at[3], pair_recv.at[3], "context", other)
    )
    dk_all[...] = jnp.zeros(dk_all.shape, BF16)
    dv_all[...] = jnp.zeros(dv_all.shape, BF16)
    pair_stat.wait_recv()

    def merged(slot):
        top = jnp.maximum(stat_mine[slot, 0:1], stat_pair[slot, 0:1])
        mine = jnp.exp2(stat_mine[slot, 0:1] - top)
        theirs = jnp.exp2(stat_pair[slot, 0:1] - top)
        inverse = 1.0 / (stat_mine[slot, 1:2] * mine + stat_pair[slot, 1:2] * theirs)
        return mine * inverse, theirs * inverse

    @pl.loop(0, 2)
    def _(step):
        slot = 1 - step
        mine, theirs = merged(slot)
        delta = (stat_mine[slot, 2:3] * mine + stat_pair[slot, 2:3] * theirs) * mine
        scaled = cot_all[slot].astype(F32) * mine
        scaled_across = scaled.astype(BF16)
        scaled_rows = scaled.T.astype(BF16)
        queries = q_all[slot]

        def back(row, query_grad):
            low = weights[slot * NX + row]
            change = matmul(tile_of(v_all, row), scaled_across, 1, 0) - delta
            score_grad = (low.astype(F32) * change).astype(BF16)
            key_term = matmul(score_grad, queries, 1, 0) * scale
            value_term = matmul(low, scaled_rows, 1, 0)
            shape = (NH, length, HD)
            at = (row // NX, lax.rem(row, NX))
            dk_all[at] = (dk_all[at].astype(F32) + key_term.reshape(shape)).astype(BF16)
            dv_all[at] = (dv_all[at].astype(F32) + value_term.reshape(shape)).astype(BF16)
            return query_grad + matmul(tile_of(k_all, row), score_grad, 0, 0)

        dq_acc[slot] = lax.fori_loop(
            0, row_of(slot) + 1, back, jnp.zeros((HD, columns), F32)
        )

    def share_out(part, recv, send_sem, recv_sem):
        return [
            send.go(
                send.build(
                    part.at[peer], recv.at[i], send_sem.at[i], recv_sem.at[i], "tensor", peer
                )
            )
            for i, peer in enumerate(peers)
        ]

    def add_up(part, recv, copies, out):
        for copy in copies:
            copy.wait_recv()
        summed = part[tensor].astype(F32)
        for i in range(len(copies)):
            summed = summed + recv[i].astype(F32)
        out[...] = summed.astype(BF16)

    strip = min(512, width)
    strips = [slice(at, at + strip) for at in range(0, width, strip)]

    def other_work():
        pair_o.wait_recv()
        mine, theirs = merged(y)
        outputs = unstack(
            (o_acc[y] * mine + o_recv[...].astype(F32) * theirs).T.astype(BF16)
        )
        for at in strips:
            term = matmul(outputs, wo[:, at], 1, 0).astype(BF16)
            for peer in range(tensors):
                part_out[peer, :, at] = term[peer * share : (peer + 1) * share]
            yield
        out_copies.extend(share_out(part_out, recv_out, out_send, out_recv))
        yield

    out_copies = []
    work = other_work()
    fold = fold_steps(
        send, place, lambda: next(work, None), dk_all, dv_all, k_sum, v_sum, grad_bufs, grad_sems
    )
    next(fold)
    dq_send[...] = dq_acc[1 - y].astype(BF16)
    pair_dq = send.go(
        send.build(dq_send, dq_recv, pair_send.at[4], pair_recv.at[4], "context", other)
    )
    next(fold)
    for _ in work:
        pass
    key_pre = rot(k_sum[...], cosines, -sines).astype(BF16)
    value_sum = v_sum[...]
    value_pre = (mix_here * value_sum).astype(BF16)
    pre_own[...] = jnp.concatenate([key_pre, value_pre], axis=1)
    row_pre = []
    for step in (2, 1, 3):
        row_pre.append(
            send.go(
                send.build(
                    pre_own, pre_far.at[step - 1], row_send.at[2 + step], row_recv.at[2 + step],
                    "context", rank_of(y, turn(x, step, NX), z),
                )
            )
        )
    gfirst_ref[...] = (mix_first * value_sum).astype(BF16)

    pair_dq.wait_recv()
    query_pre = unstack(
        rot(
            (dq_acc[y] + dq_recv[...].astype(F32)).T * scale, spread(cosines), -spread(sines)
        ).astype(BF16)
    )
    for at in strips:
        term = matmul(query_pre, wq[at, :], 1, 1) + matmul(pre_own[...], wkv[at, :], 1, 1)
        term = term.astype(BF16)
        for peer in range(tensors):
            part_in[peer, :, at] = term[peer * share : (peer + 1) * share]

    in_copies = share_out(part_in, recv_in, in_send, in_recv)
    many, rows = w_part.shape[1], w_part.shape[2]

    def term_of(side, pre):
        return matmul(side.reshape(NY * many * rows, length), pre, 1, 0)

    for copy in row_x + row_pre:
        copy.wait_recv()
    summed = term_of(xt[:, x], pre_own[...])
    for i in range(NX - 1):
        summed = summed + term_of(xt_far[i], pre_far[i])
    w_part[...] = summed.astype(BF16).reshape(w_part.shape)
    earlier = Sender()
    earlier.started, send.started = send.started, []
    ring = []
    for step in (4, 3, 5, 2, 6, 1, 7):
        goal = turn(z, step, NZ)
        ring.append(
            send.go(
                send.build(
                    w_part.at[:, goal], w_far.at[step - 1], ring_send.at[step - 1],
                    ring_recv.at[step - 1], "context", rank_of(y, x, goal),
                )
            )
        )
    add_up(part_out, recv_out, out_copies, attn_ref)
    earlier.finish()
    add_up(part_in, recv_in, in_copies, gin_ref)
    for copy in ring:
        copy.wait_recv()

    def strip_sum(half):
        total = w_part[half, z].astype(F32)
        for i in range(NZ - 1):
            total = total + w_far[i, half].astype(F32)
        return total

    w_low[...] = strip_sum(1 - y).astype(BF16)
    pair_w = send.go(
        send.build(
            w_low, w_last, pair_send.at[5], pair_recv.at[5], "context", rank_of(1 - y, x, z)
        )
    )
    weight = strip_sum(y)
    pair_w.wait_recv()
    weight = weight + w_last[...].astype(F32)
    gwk_ref[...] = weight[:, :HD]
    gwv_ref[...] = weight[:, HD:]
    send.finish()


def store_kernel(*refs):
    count = len(refs) // 2
    for i in range(count):
        refs[count + i][...] = refs[i][...]


def rope_tables(positions, head_width):
    half_width = head_width // 2
    exponent = jnp.arange(half_width, dtype=F32) * (2.0 / head_width)
    frequency = jnp.power(jnp.float32(THETA), -exponent)
    angles = positions.astype(F32)[:, None] * frequency[None, :]
    return (jnp.cos(angles), jnp.sin(angles))


def shards(hidden_in, value_first, w_query, w_key, w_value, w_out, value_mix, grad_out):
    tensors = lax.axis_size("tensor")
    length, width = hidden_in.shape[1:]
    features = w_query.shape[1]
    columns = features // HD * length
    share = length // tensors
    rows = width // (NY * NX * NZ)
    block_rows = lax.axis_index("context") * length + jnp.arange(length, dtype=jnp.int32)
    cosines, sines = rope_tables(block_rows, HD)
    tables = jnp.concatenate(
        [
            jnp.concatenate([cosines, cosines], axis=1),
            jnp.concatenate([-sines, sines], axis=1),
            jnp.broadcast_to(value_mix[:, :1], (2, HD)),
            jnp.zeros((6, HD), F32),
        ],
        axis=0,
    )
    vmem = pl.BlockSpec(memory_space=pltpu.VMEM)
    hbm = pl.BlockSpec(memory_space=pl.ANY)
    dma = pltpu.SemaphoreType.DMA

    def low(*shape):
        return pltpu.VMEM(shape, BF16)

    def full(*shape):
        return pltpu.VMEM(shape, F32)

    def fold_room(ends, count):
        return (
            low(4, 4, NX, count, HD), low(NY, ends, count, HD), low(NY, ends, 2, count, HD),
            low(4, 4, count, HD), low(NX, NY, count, HD), low(NY, ends, count, HD),
            low(3, NY, count, HD), low(2, NY, count, HD), low(2, count, HD),
        )

    others = (max(tensors - 1, 1),)
    scratch = [
        low(length, width), low(width, features), low(width, 2 * HD),
        low(features, width), low(length, width), low(NY, NX, NZ * rows, length), low(length, HD),
        low(length, HD), low(NY, NX, NH, length, HD), low(NY, NX, NH, length, HD),
        low(2, columns, HD), low(2, HD, columns), low(3 * NX, NH * length, columns),
        full(2, HD, columns), full(2, HD, columns), low(HD, columns), low(HD, columns),
        low(HD, columns), low(HD, columns), full(2, 8, columns), full(2, 8, columns),
        low(NY, NX, NH, length, HD), low(NY, NX, NH, length, HD), full(length, HD),
        full(length, HD), low(tensors, share, width), low(others[0], share, width),
        low(tensors, share, width), low(others[0], share, width),
        low(NX - 1, NY, NZ * rows, length), low(length, 2 * HD), low(NX - 1, length, 2 * HD),
        low(NY, NZ, rows, 2 * HD), low(NZ - 1, NY, rows, 2 * HD), low(rows, 2 * HD),
        low(rows, 2 * HD),
        fold_room(NH, length), dma((6,)),
        (dma((2,)), dma((2,)), dma((3,)), dma((3,)), dma((4, 4)), dma((4, 4)), dma((4, 4, NX)),
         dma((4, 4, NX)), dma((NY, NH, 2)), dma((NY, NH, 2)), dma((NY, NH)), dma((NY, NH))),
    ]

    def fold_sems(ends):
        return (
            dma((4, 4, NX)), dma((4, 4, NX)), dma((NY, ends)), dma((NY, ends)),
            dma((NY, ends, 2)), dma((NY, ends, 2)), dma((4, 4)), dma((4, 4)), dma((3,)), dma((3,)),
            dma((2,)), dma((2,)),
        )

    scratch += [fold_sems(NH), dma((6,)), dma((6,)), dma((NZ - 1,)), dma((NZ - 1,))]
    scratch += [dma((6,)), dma((6,))] + [dma(others)] * 6
    results = pl.pallas_call(
        block_kernel,
        out_shape=(
            jax.ShapeDtypeStruct((share, width), BF16),
            jax.ShapeDtypeStruct((share, width), BF16),
            jax.ShapeDtypeStruct((length, HD), BF16),
            jax.ShapeDtypeStruct((rows, HD), F32),
            jax.ShapeDtypeStruct((rows, HD), F32),
        ),
        in_specs=[hbm, vmem, hbm, hbm, hbm, hbm, hbm, vmem],
        out_specs=(vmem,) * 5,
        scratch_shapes=scratch,
        compiler_params=pltpu.CompilerParams(
            collective_id=1, has_side_effects=True, vmem_limit_bytes=56 * 2**20
        ),
        name="attention_block",
    )(
        hidden_in.reshape(length, width), value_first.reshape(length, HD), w_query, w_key, w_value,
        w_out, grad_out.reshape(share, width), tables,
    )
    attn_out, grad_in, grad_first, key_weight, value_weight = pl.pallas_call(
        store_kernel,
        out_shape=tuple(jax.ShapeDtypeStruct(part.shape, part.dtype) for part in results),
        in_specs=[vmem] * len(results),
        out_specs=(vmem,) * len(results),
        name="store_results",
    )(*results)
    return (
        attn_out.reshape(1, share, width),
        grad_in.reshape(1, share, width),
        grad_first.reshape(1, length, HD),
        key_weight,
        value_weight,
    )


def solution(mesh):
    return jax.shard_map(
        shards,
        mesh=mesh,
        in_specs=(
            P("context", None, None),
            P("context", None, "tensor"),
            P(None, "tensor"),
            P(None, "tensor"),
            P(None, "tensor"),
            P("tensor", None),
            P(None, "tensor"),
            P("context", "tensor", None),
        ),
        out_specs=(
            P("context", "tensor", None),
            P("context", "tensor", None),
            P("context", None, "tensor"),
            P("context", "tensor"),
            P("context", "tensor"),
        ),
        check_vma=False,
    )
```

```python
import jax
import jax.numpy as jnp
from jax import lax
from jax.experimental import pallas as pl
from jax.experimental.pallas import tpu as pltpu
from jax.sharding import PartitionSpec as P

HD = 128
THETA = 500000.0
LOG2E = 1.4426950408889634
NEGATIVE = -1e30
NY, NX, NZ = 2, 4, 8
NH = NZ // 2
F32, BF16 = jnp.float32, jnp.bfloat16

CHAINS = ((1, 0, 4, 2), (1, 1, 3, 1), (-1, 1, 4, 2), (-1, 0, 3, 1))
ORDER = (0, 2, 1, 3)
ARRIVE = ((0, 3), (1, 2))


def rank_of(y, x, z):
    return (y * NX + x) * NZ + z


def turn(value, step, count):
    return lax.rem(value + (step + count), count)


def when(condition, action):
    if condition is True:
        action()
    else:
        pl.when(condition)(action)


def matmul(left, right, left_dim, right_dim):
    return lax.dot_general(
        left, right, (((left_dim,), (right_dim,)), ((), ())), preferred_element_type=F32
    )


def add_into(target, term):
    target[...] = (target[...].astype(F32) + term[...].astype(F32)).astype(BF16)


class Sender:
    def __init__(self):
        self.started = []

    def build(self, source, target, send_sem, recv_sem, axis, rank):
        return pltpu.make_async_remote_copy(
            src_ref=source,
            dst_ref=target,
            send_sem=send_sem,
            recv_sem=recv_sem,
            device_id={axis: rank},
            device_id_type=pl.DeviceIdType.MESH,
        )

    def go(self, copy, condition=True):
        copy.start()
        self.started.append((condition, copy))
        return copy

    def finish(self):
        for condition, copy in self.started:
            when(condition, copy.wait_send)


class Place:
    def __init__(self):
        rank = lax.axis_index("context")
        self.rank = rank
        self.y, self.x, self.z = rank // (NX * NZ), (rank // NZ) % NX, rank % NZ
        self.z_ring = [lax.rem(self.z + step, NZ) for step in range(NZ)]
        self.x_ring = [lax.rem(self.x + step, NX) for step in range(NX)]
        self.halves = [at // 2 for at in self.z_ring]
        even = lax.rem(self.z + self.y, 2) == 0
        self.parity = (even, jnp.logical_not(even))

    def z_at(self, step):
        return self.z_ring[step % NZ]

    def x_at(self, step):
        return self.x_ring[step % NX]

    def half(self, step):
        return self.halves[step % NZ]

    def holds(self, step):
        return self.parity[step % 2]


def gather_steps(send, place, k_own, v_own, k_all, v_all, sems):
    y, x, z = place.y, place.x, place.z
    y_send, y_recv, kx_send, kx_recv, vz_send, vz_recv, kz_send, kz_recv = sems[:8]
    vx_send, vx_recv, vf_send, vf_recv = sems[8:]
    slot = place.half(0)
    partner = rank_of(1 - y, x, z)
    lends = place.holds(1)
    pairs = [
        send.build(own, whole.at[y, x, slot], y_send.at[i], y_recv.at[i], "context", partner)
        for i, (own, whole) in enumerate(((k_own, k_all), (v_own, v_all)))
    ]

    def lend():
        for copy in pairs:
            copy.start()

    def keep():
        k_all[y, x, slot] = k_own[...]
        v_all[y, x, slot] = v_own[...]

    pl.when(lends)(lend)
    pl.when(place.holds(0))(keep)
    send.started += [(lends, copy) for copy in pairs]

    kx = {}
    for step in (1, 3, 2):
        part = k_all.at[:, x, slot]
        kx[step] = send.build(
            part, part, kx_send.at[step - 1], kx_recv.at[step - 1], "context",
            rank_of(y, place.x_at(step), z),
        )
    rows = (0, 1, 3, 2)

    def kz_copy(chain, hop, part_at):
        way, half, _, _ = CHAINS[chain]
        part = k_all.at[half, place.x_at(rows[part_at]), place.half(-way * hop)]
        return send.build(
            part, part, kz_send.at[chain, hop, part_at], kz_recv.at[chain, hop, part_at],
            "context", rank_of(y, x, place.z_at(way)),
        )

    def kz(hop, part_at):
        if hop == 0 and part_at:
            pl.when(place.holds(0))(kx[NX - rows[part_at]].wait_recv)
        for chain in ORDER:
            if hop < CHAINS[chain][2]:
                condition = place.holds(-CHAINS[chain][0] * hop)
                copy = kz_copy(chain, hop, part_at)

                def act():
                    if hop:
                        kz_copy(chain, hop - 1, part_at).wait_recv()
                    copy.start()

                when(condition, act)
                send.started.append((condition, copy))

    def vz_copy(chain, hop):
        way, half, _, _ = CHAINS[chain]
        part = v_all.at[half, x, place.half(-way * hop)]
        return send.build(
            part, part, vz_send.at[chain, hop], vz_recv.at[chain, hop], "context",
            rank_of(y, x, place.z_at(way)),
        )

    def vx_copy(half, at, way):
        part = v_all.at[half, x, at]
        side = 0 if way > 0 else 1
        return send.build(
            part, part, vx_send.at[half, at, side], vx_recv.at[half, at, side], "context",
            rank_of(y, place.x_at(way), z),
        )

    def vf_copy(half, at):
        way = 1 if half == 0 else -1
        part = v_all.at[half, place.x_at(-way), at]
        return send.build(
            part, part, vf_send.at[half, at], vf_recv.at[half, at], "context",
            rank_of(y, place.x_at(way), z),
        )

    def pieces(distance):
        if distance == 0:
            return [(None, place.holds(0), half, slot) for half in range(NY)]
        found = []
        for chain in ORDER:
            way, half, hops, _ = CHAINS[chain]
            if distance <= hops:
                step = -way * distance
                found.append((chain, place.holds(step), half, place.half(step)))
        return found

    def v_round(distance):
        for chain, condition, half, at in pieces(distance):
            copies = [vx_copy(half, at, 1), vx_copy(half, at, -1)]
            if chain is None:
                copies += [vz_copy(c, 0) for c in ORDER if CHAINS[c][1] == half]
            elif distance < CHAINS[chain][2]:
                copies.insert(0, vz_copy(chain, distance))

            def act():
                if chain is not None:
                    vz_copy(chain, distance - 1).wait_recv()
                for copy in copies:
                    copy.start()

            when(condition, act)
            send.started += [(condition, copy) for copy in copies]

    def forward(distance):
        for _, condition, half, at in pieces(distance):
            copy = vf_copy(half, at)

            def act():
                vx_copy(half, at, 1 if half == 0 else -1).wait_recv()
                copy.start()

            when(condition, act)
            send.started.append((condition, copy))

    def finish():
        for distance in range(5):
            for _, condition, half, at in pieces(distance):

                def act():
                    vx_copy(half, at, -1 if half == 0 else 1).wait_recv()
                    vf_copy(half, at).wait_recv()

                when(condition, act)
        for chain in ORDER:
            way, _, hops, _ = CHAINS[chain]
            condition = place.holds(-way * hops)

            def act():
                for part_at in range(NX):
                    kz_copy(chain, hops - 1, part_at).wait_recv()

            when(condition, act)

    yield

    def start_rows():
        for copy in pairs:
            copy.wait_recv()
        for copy in kx.values():
            copy.start()

    pl.when(place.holds(0))(start_rows)
    send.started += [(place.holds(0), copy) for copy in kx.values()]
    v_round(0)
    kz(0, 0)
    v_round(1)
    kz(0, 1)
    kz(1, 0)
    forward(0)
    yield
    v_round(2)
    kz(0, 2)
    kz(1, 1)
    kz(2, 0)
    forward(1)
    yield
    v_round(3)
    kz(0, 3)
    kz(1, 2)
    kz(2, 1)
    kz(3, 0)
    forward(2)
    v_round(4)
    kz(1, 3)
    kz(2, 2)
    kz(3, 1)
    forward(3)
    kz(2, 3)
    kz(3, 2)
    forward(4)
    kz(3, 3)
    yield
    finish()
    yield


def fold_steps(send, place, idle, a_in, b_in, a_out, b_out, bufs, sems):
    y, x, z = place.y, place.x, place.z

    az_buf, far_buf, near_buf, bz_buf, a_sum, b_sum, ax_buf, low, y_buf = bufs
    az_send, az_recv, far_send, far_recv, near_send, near_recv, bz_send, bz_recv = sems[:8]
    ax_send, ax_recv, y_send, y_recv = sems[8:]
    slot = place.half(0)
    rows = (2, 1, 3, 0)

    def az_copy(chain, hop, part_at):
        way, half, hops, _ = CHAINS[chain]
        own = a_in.at[half, place.x_at(rows[part_at]), place.half(way * (hops - hop))]
        source = az_buf.at[chain, hop - 1, part_at] if hop else own
        copy = send.build(
            source, az_buf.at[chain, hop, part_at], az_send.at[chain, hop, part_at],
            az_recv.at[chain, hop, part_at], "context", rank_of(y, x, place.z_at(way)),
        )
        return own, copy

    def az(hop, part_at):
        for chain in ORDER:
            way, _, hops, _ = CHAINS[chain]
            if hop < hops:
                condition = place.holds(way * (hops - hop))
                own, copy = az_copy(chain, hop, part_at)

                def act():
                    if hop:
                        az_copy(chain, hop - 1, part_at)[1].wait_recv()
                        add_into(az_buf.at[chain, hop - 1, part_at], own)
                    copy.start()

                when(condition, act)
                send.started.append((condition, copy))

    def ax_copy(step):
        goal = place.x_at(step)
        return send.build(
            a_sum.at[goal], ax_buf.at[step - 1], ax_send.at[step - 1], ax_recv.at[step - 1],
            "context", rank_of(y, goal, z),
        )

    def a_end(part_at):
        row = place.x_at(rows[part_at])

        def act():
            for half in range(NY):
                summed = a_in[half, row, slot].astype(F32)
                for chain in ARRIVE[half]:
                    hops = CHAINS[chain][2]
                    az_copy(chain, hops - 1, part_at)[1].wait_recv()
                    summed = summed + az_buf[chain, hops - 1, part_at].astype(F32)
                a_sum[row, half] = summed.astype(BF16)
            if rows[part_at]:
                ax_copy(rows[part_at]).start()

        when(place.holds(0), act)
        if rows[part_at]:
            send.started.append((place.holds(0), ax_copy(rows[part_at])))

    def pieces(distance):
        if distance == 0:
            return [(None, place.holds(0), half, slot) for half in range(NY)]
        found = []
        for chain in ORDER:
            way, half, hops, _ = CHAINS[chain]
            if distance <= hops:
                step = way * distance
                found.append((chain, place.holds(step), half, place.half(step)))
        return found

    def outward(half):
        return 1 if half == 0 else -1

    def far_copy(half, at):
        way = outward(half)
        return send.build(
            b_in.at[half, place.x_at(2), at], far_buf.at[half, at], far_send.at[half, at],
            far_recv.at[half, at], "context", rank_of(y, place.x_at(way), z),
        )

    def near_copy(half, at, way):
        side = 0 if way > 0 else 1
        goal = place.x_at(way)
        source = far_buf.at[half, at] if way == outward(half) else b_in.at[half, goal, at]
        return send.build(
            source, near_buf.at[half, at, side], near_send.at[half, at, side],
            near_recv.at[half, at, side], "context", rank_of(y, goal, z),
        )

    def b_start(distance):
        for _, condition, half, at in pieces(distance):
            copies = [far_copy(half, at), near_copy(half, at, -outward(half))]

            def act():
                for copy in copies:
                    copy.start()

            when(condition, act)
            send.started += [(condition, copy) for copy in copies]

    def b_middle(distance):
        for _, condition, half, at in pieces(distance):
            copy = near_copy(half, at, outward(half))

            def act():
                far_copy(half, at).wait_recv()
                add_into(far_buf.at[half, at], b_in.at[half, place.x_at(outward(half)), at])
                copy.start()

            when(condition, act)
            send.started.append((condition, copy))

    def bz_copy(chain, hop):
        way, half, hops, _ = CHAINS[chain]
        own = b_sum.at[half, place.half(way * (hops - hop))]
        return send.build(
            own, bz_buf.at[chain, hop], bz_send.at[chain, hop], bz_recv.at[chain, hop],
            "context", rank_of(y, x, place.z_at(way)),
        )

    def b_end(distance):
        for chain, condition, half, at in pieces(distance):
            if chain is not None:
                hop = CHAINS[chain][2] - distance

            def act():
                summed = b_in[half, x, at].astype(F32)
                for way in (1, -1):
                    near_copy(half, at, way).wait_recv()
                    summed = summed + near_buf[half, at, 0 if way > 0 else 1].astype(F32)
                if chain is None:
                    arrivals = [(c, CHAINS[c][2] - 1) for c in ARRIVE[half]]
                else:
                    arrivals = [(chain, hop - 1)] if hop else []
                for other, at_hop in arrivals:
                    bz_copy(other, at_hop).wait_recv()
                    summed = summed + bz_buf[other, at_hop].astype(F32)
                if chain is None:
                    low[1, half] = summed.astype(BF16)
                else:
                    b_sum[half, at] = summed.astype(BF16)
                    bz_copy(chain, hop).start()

            when(condition, act)
            if chain is not None:
                send.started.append((condition, bz_copy(chain, hop)))

    partner = rank_of(1 - y, x, z)
    pairs = [
        send.build(
            low.at[i, 1 - y], y_buf.at[i], y_send.at[i], y_recv.at[i], "context", partner
        )
        for i in range(2)
    ]

    def hand_over(i):
        when(place.holds(0), pairs[i].start)
        send.started.append((place.holds(0), pairs[i]))

    def close(i, out):
        def keep():
            out[...] = low[i, y].astype(F32)

        def take():
            pairs[i].wait_recv()
            out[...] = y_buf[i].astype(F32)

        pl.when(place.holds(0))(keep)
        pl.when(place.holds(1))(take)

    def a_row():
        for step in (1, 2, 3):
            ax_copy(step).wait_recv()
        summed = a_sum[x].astype(F32)
        for step in range(3):
            summed = summed + ax_buf[step].astype(F32)
        low[0] = summed.astype(BF16)

    b_start(4)
    b_start(3)
    az(0, 0)
    az(0, 1)
    b_start(2)
    az(0, 2)
    b_start(1)
    az(0, 3)
    b_start(0)
    yield
    for work, arguments in (
        (b_middle, (4,)), (b_middle, (3,)), (az, (1, 0)), (az, (1, 1)), (b_middle, (2,)),
        (b_end, (4,)), (b_end, (3,)), (az, (1, 2)), (az, (2, 0)), (b_middle, (1,)), (az, (1, 3)),
        (az, (2, 1)), (b_middle, (0,)), (b_end, (2,)), (az, (3, 0)), (az, (2, 2)), (az, (3, 1)),
        (b_end, (1,)), (a_end, (0,)), (az, (2, 3)), (az, (3, 2)), (a_end, (1,)), (az, (3, 3)),
        (a_end, (2,)), (b_end, (0,)),
    ):
        work(*arguments)
        idle()
    hand_over(1)
    a_end(3)
    when(place.holds(0), a_row)
    hand_over(0)
    close(1, b_out)
    close(0, a_out)
    yield


def block_kernel(
    x_hbm, first_ref, wq_hbm, wk_hbm, wv_hbm, wo_hbm, g_hbm, table_ref,
    attn_ref, gin_ref, gfirst_ref, gwk_ref, gwv_ref,
    x_buf, wq, wkv, wo, g_all, xt, k_own, v_own, k_all, v_all, q_all, cot_all, weights,
    o_acc, dq_acc, o_send, o_recv, dq_send, dq_recv, stat_mine, stat_pair, dk_all, dv_all,
    k_sum, v_sum, part_out, recv_out, part_in, recv_in, xt_far,
    pre_own, pre_far, w_part, w_far, w_low, w_last, grad_bufs, local_sem, gather_sems, grad_sems,
    row_send, row_recv, ring_send, ring_recv,
    pair_send, pair_recv, g_send, g_recv, out_send, out_recv, in_send, in_recv,
):
    place = Place()
    y, x, z = place.y, place.x, place.z
    tensor, tensors = lax.axis_index("tensor"), lax.axis_size("tensor")
    length, width = x_buf.shape
    columns = q_all.shape[1]
    heads = columns // length
    share = length // tensors
    tile = NH * length
    scale = HD ** (-0.5)
    factor = scale * LOG2E

    other = rank_of(1 - y, NX - 1 - x, z)
    peers = [lax.rem(tensor + step, tensors) for step in range(1, tensors)]
    my_rows = pl.ds(pl.multiple_of(tensor * share, share), share)

    loads = [
        pltpu.make_async_copy(source, target, local_sem.at[i])
        for i, (source, target) in enumerate(
            ((x_hbm, x_buf), (wk_hbm, wkv.at[:, :HD]), (wv_hbm, wkv.at[:, HD:]), (g_hbm, g_all.at[my_rows]), (wq_hbm, wq),
             (wo_hbm, wo))
        )
    ]
    for copy in loads[:5]:
        copy.start()
    barrier = pltpu.get_barrier_semaphore()
    ranks = [rank_of(1 - y, x, z), rank_of(y, x, turn(z, 1, NZ)), rank_of(y, x, turn(z, -1, NZ))]
    ranks += [rank_of(y, turn(x, step, NX), z) for step in (1, 2, 3)]
    ranks += [rank_of(y, x, turn(z, step, NZ)) for step in range(2, NZ - 1)]
    ranks += [other]
    for who in [{"context": at} for at in ranks] + [{"tensor": at} for at in peers]:
        pl.semaphore_signal(barrier, inc=1, device_id=who, device_id_type=pl.DeviceIdType.MESH)

    cosines, sines = table_ref[:length], table_ref[length : 2 * length]
    mix_here = table_ref[2 * length : 2 * length + 1]
    mix_first = table_ref[2 * length + 1 : 2 * length + 2]

    def spread(table):
        return jnp.concatenate([table] * heads, axis=0)

    def swap(field):
        return jnp.concatenate([field[:, HD // 2 :], field[:, : HD // 2]], axis=1)

    def rot(field, cosine_part, sine_part):
        return field * cosine_part + swap(field) * sine_part

    def stack(field):
        return jnp.concatenate([field[:, h * HD : (h + 1) * HD] for h in range(heads)], axis=0)

    def unstack(field):
        return jnp.concatenate(
            [field[h * length : (h + 1) * length] for h in range(heads)], axis=1
        )

    for copy in loads[:3]:
        copy.wait()
    loads[5].start()
    projected = matmul(x_buf[...], wkv[...], 1, 0)
    k_own[...] = rot(projected[:, :HD], cosines, sines).astype(BF16)
    v_own[...] = (
        mix_here * projected[:, HD:] + mix_first * first_ref[...].astype(F32)
    ).astype(BF16)
    pl.semaphore_wait(barrier, len(ranks) + len(peers))

    send = Sender()
    gather = gather_steps(send, place, k_own, v_own, k_all, v_all, gather_sems)
    next(gather)
    loads[3].wait()
    g_copies = [
        send.go(
            send.build(
                g_all.at[my_rows], g_all.at[my_rows], g_send.at[i], g_recv.at[i], "tensor", peer
            )
        )
        for i, peer in enumerate(peers)
    ]
    loads[4].wait()
    q_all[y] = rot(
        stack(matmul(x_buf[...], wq[...], 1, 0)), spread(cosines), spread(sines)
    ).astype(BF16)
    pair_q = send.go(
        send.build(q_all.at[y], q_all.at[y], pair_send.at[0], pair_recv.at[0], "context", other)
    )
    for _ in range(3):
        next(gather)
    for copy in g_copies:
        copy.wait_recv()
    loads[5].wait()
    cotangent = matmul(wo[...], g_all[...], 1, 1).astype(BF16)
    for h in range(heads):
        cot_all[y, :, h * length : (h + 1) * length] = cotangent[h * HD : (h + 1) * HD]
    pair_cot = send.go(
        send.build(cot_all.at[y], cot_all.at[y], pair_send.at[1], pair_recv.at[1], "context", other)
    )
    xt[...] = x_buf[...].T.reshape(xt.shape)
    next(gather)
    row_x = []
    for step in (1, 3, 2):
        goal = turn(x, step, NX)
        row_x.append(
            send.go(
                send.build(
                    xt.at[:, goal], xt_far.at[step - 1], row_send.at[step - 1],
                    row_recv.at[step - 1], "context", rank_of(y, goal, z),
                )
            )
        )
    pair_q.wait_recv()

    key_in_tile = lax.broadcasted_iota(jnp.int32, (tile, columns), 0)
    key_in_tile = (2 * (key_in_tile // length) + y) * length + lax.rem(key_in_tile, length)
    query_in_block = lax.rem(lax.broadcasted_iota(jnp.int32, (tile, columns), 1), length)
    def row_of(slot):
        return jnp.where(slot == y, y * NX + x, slot * NX + NX - 1 - x)

    def tile_of(ref, row):
        return ref[row // NX, lax.rem(row, NX)].reshape(tile, HD)

    def forward(slot):
        last = row_of(slot)
        visible = key_in_tile <= query_in_block + z * length
        queries = q_all[slot].astype(F32).T.astype(BF16)

        def scores(row):
            return matmul(tile_of(k_all, row), queries, 1, 0)

        def max_step(row, current):
            return jnp.maximum(current, jnp.max(scores(row), axis=0, keepdims=True))

        top = jnp.max(jnp.where(visible, scores(last), NEGATIVE), axis=0, keepdims=True)
        top = lax.fori_loop(0, last, max_step, top) * factor

        def weigh(row, current, masked):
            totals, output = current
            exponent = scores(row) * factor - top
            if masked:
                exponent = jnp.where(visible, exponent, NEGATIVE)
            weight = jnp.exp2(exponent)
            totals = totals + jnp.sum(weight, axis=0, keepdims=True)
            low = weight.astype(BF16)
            weights[slot * NX + row] = low
            return totals, output + matmul(tile_of(v_all, row), low, 0, 0)

        start = (jnp.zeros((1, columns), F32), jnp.zeros((HD, columns), F32))
        start = weigh(last, start, True)
        totals, output = lax.fori_loop(
            0, last, lambda row, current: weigh(row, current, False), start
        )
        stat_mine[slot, 0:1] = top
        stat_mine[slot, 1:2] = totals
        o_acc[slot] = output

    pair_stat = {}
    for slot in (1, 0):
        forward(slot)
        if slot == 1:
            pair_cot.wait_recv()
        stat_mine[slot, 2:3] = jnp.sum(
            cot_all[slot].astype(F32) * o_acc[slot], axis=0, keepdims=True
        )
        pair_stat[slot] = send.go(
            send.build(
                stat_mine.at[slot], stat_pair.at[slot], pair_send.at[5 + slot],
                pair_recv.at[5 + slot], "context", other,
            )
        )
    o_send[...] = o_acc[1 - y].astype(BF16)
    pair_o = send.go(
        send.build(o_send, o_recv, pair_send.at[3], pair_recv.at[3], "context", other)
    )
    dk_all[...] = jnp.zeros(dk_all.shape, BF16)
    dv_all[...] = jnp.zeros(dv_all.shape, BF16)

    def merged(slot):
        top = jnp.maximum(stat_mine[slot, 0:1], stat_pair[slot, 0:1])
        mine = jnp.exp2(stat_mine[slot, 0:1] - top)
        theirs = jnp.exp2(stat_pair[slot, 0:1] - top)
        inverse = 1.0 / (stat_mine[slot, 1:2] * mine + stat_pair[slot, 1:2] * theirs)
        return mine * inverse, theirs * inverse

    def backward(slot):
        mine, theirs = merged(slot)
        delta = (stat_mine[slot, 2:3] * mine + stat_pair[slot, 2:3] * theirs) * mine
        scaled = cot_all[slot].astype(F32) * mine
        scaled_across = scaled.astype(BF16)
        scaled_rows = scaled.T.astype(BF16)
        queries = q_all[slot]

        def back(row, query_grad):
            low = weights[slot * NX + row]
            change = matmul(tile_of(v_all, row), scaled_across, 1, 0) - delta
            score_grad = (low.astype(F32) * change).astype(BF16)
            key_term = matmul(score_grad, queries, 1, 0) * scale
            value_term = matmul(low, scaled_rows, 1, 0)
            shape = (NH, length, HD)
            at = (row // NX, lax.rem(row, NX))
            dk_all[at] = (dk_all[at].astype(F32) + key_term.reshape(shape)).astype(BF16)
            dv_all[at] = (dv_all[at].astype(F32) + value_term.reshape(shape)).astype(BF16)
            return query_grad + matmul(tile_of(k_all, row), score_grad, 0, 0)

        dq_acc[slot] = lax.fori_loop(
            0, row_of(slot) + 1, back, jnp.zeros((HD, columns), F32)
        )

    for slot in (1, 0):
        pair_stat[slot].wait_recv()
        backward(slot)

    def share_out(part, recv, send_sem, recv_sem):
        return [
            send.go(
                send.build(
                    part.at[peer], recv.at[i], send_sem.at[i], recv_sem.at[i], "tensor", peer
                )
            )
            for i, peer in enumerate(peers)
        ]

    def add_up(part, recv, copies, out):
        for copy in copies:
            copy.wait_recv()
        summed = part[tensor].astype(F32)
        for i in range(len(copies)):
            summed = summed + recv[i].astype(F32)
        out[...] = summed.astype(BF16)

    strip = min(512, width)
    strips = [slice(at, at + strip) for at in range(0, width, strip)]

    def other_work():
        pair_o.wait_recv()
        mine, theirs = merged(y)
        outputs = unstack(
            (o_acc[y] * mine + o_recv[...].astype(F32) * theirs).T.astype(BF16)
        )
        for at in strips:
            term = matmul(outputs, wo[:, at], 1, 0).astype(BF16)
            for peer in range(tensors):
                part_out[peer, :, at] = term[peer * share : (peer + 1) * share]
            yield
        out_copies.extend(share_out(part_out, recv_out, out_send, out_recv))
        yield

    out_copies = []
    work = other_work()
    fold = fold_steps(
        send, place, lambda: next(work, None), dk_all, dv_all, k_sum, v_sum, grad_bufs, grad_sems
    )
    next(fold)
    dq_send[...] = dq_acc[1 - y].astype(BF16)
    pair_dq = send.go(
        send.build(dq_send, dq_recv, pair_send.at[4], pair_recv.at[4], "context", other)
    )
    next(fold)
    for _ in work:
        pass
    key_pre = rot(k_sum[...], cosines, -sines).astype(BF16)
    value_sum = v_sum[...]
    value_pre = (mix_here * value_sum).astype(BF16)
    pre_own[...] = jnp.concatenate([key_pre, value_pre], axis=1)
    row_pre = []
    for step in (2, 1, 3):
        row_pre.append(
            send.go(
                send.build(
                    pre_own, pre_far.at[step - 1], row_send.at[2 + step], row_recv.at[2 + step],
                    "context", rank_of(y, turn(x, step, NX), z),
                )
            )
        )
    gfirst_ref[...] = (mix_first * value_sum).astype(BF16)

    pair_dq.wait_recv()
    query_pre = unstack(
        rot(
            (dq_acc[y] + dq_recv[...].astype(F32)).T * scale, spread(cosines), -spread(sines)
        ).astype(BF16)
    )
    for at in strips:
        term = matmul(query_pre, wq[at, :], 1, 1) + matmul(pre_own[...], wkv[at, :], 1, 1)
        term = term.astype(BF16)
        for peer in range(tensors):
            part_in[peer, :, at] = term[peer * share : (peer + 1) * share]

    in_copies = share_out(part_in, recv_in, in_send, in_recv)
    many, rows = w_part.shape[1], w_part.shape[2]

    def term_of(side, pre):
        return matmul(side.reshape(NY * many * rows, length), pre, 1, 0)

    for copy in row_x + row_pre:
        copy.wait_recv()
    summed = term_of(xt[:, x], pre_own[...])
    for i in range(NX - 1):
        summed = summed + term_of(xt_far[i], pre_far[i])
    w_part[...] = summed.astype(BF16).reshape(w_part.shape)
    earlier = Sender()
    earlier.started, send.started = send.started, []
    ring = []
    for step in (4, 3, 5, 2, 6, 1, 7):
        goal = turn(z, step, NZ)
        ring.append(
            send.go(
                send.build(
                    w_part.at[:, goal], w_far.at[step - 1], ring_send.at[step - 1],
                    ring_recv.at[step - 1], "context", rank_of(y, x, goal),
                )
            )
        )
    add_up(part_out, recv_out, out_copies, attn_ref)
    earlier.finish()
    add_up(part_in, recv_in, in_copies, gin_ref)
    for copy in ring:
        copy.wait_recv()

    def strip_sum(half):
        total = w_part[half, z].astype(F32)
        for i in range(NZ - 1):
            total = total + w_far[i, half].astype(F32)
        return total

    w_low[...] = strip_sum(1 - y).astype(BF16)
    pair_w = send.go(
        send.build(
            w_low, w_last, pair_send.at[2], pair_recv.at[2], "context", rank_of(1 - y, x, z)
        )
    )
    weight = strip_sum(y)
    pair_w.wait_recv()
    weight = weight + w_last[...].astype(F32)
    gwk_ref[...] = weight[:, :HD]
    gwv_ref[...] = weight[:, HD:]
    send.finish()


def store_kernel(*refs):
    count = len(refs) // 2
    for i in range(count):
        refs[count + i][...] = refs[i][...]


def rope_tables(positions, head_width):
    half_width = head_width // 2
    exponent = jnp.arange(half_width, dtype=F32) * (2.0 / head_width)
    frequency = jnp.power(jnp.float32(THETA), -exponent)
    angles = positions.astype(F32)[:, None] * frequency[None, :]
    return (jnp.cos(angles), jnp.sin(angles))


def shards(hidden_in, value_first, w_query, w_key, w_value, w_out, value_mix, grad_out):
    tensors = lax.axis_size("tensor")
    length, width = hidden_in.shape[1:]
    features = w_query.shape[1]
    columns = features // HD * length
    share = length // tensors
    rows = width // (NY * NX * NZ)
    block_rows = lax.axis_index("context") * length + jnp.arange(length, dtype=jnp.int32)
    cosines, sines = rope_tables(block_rows, HD)
    tables = jnp.concatenate(
        [
            jnp.concatenate([cosines, cosines], axis=1),
            jnp.concatenate([-sines, sines], axis=1),
            jnp.broadcast_to(value_mix[:, :1], (2, HD)),
            jnp.zeros((6, HD), F32),
        ],
        axis=0,
    )
    vmem = pl.BlockSpec(memory_space=pltpu.VMEM)
    hbm = pl.BlockSpec(memory_space=pl.ANY)
    dma = pltpu.SemaphoreType.DMA

    def low(*shape):
        return pltpu.VMEM(shape, BF16)

    def full(*shape):
        return pltpu.VMEM(shape, F32)

    def fold_room(ends, count):
        return (
            low(4, 4, NX, count, HD), low(NY, ends, count, HD), low(NY, ends, 2, count, HD),
            low(4, 4, count, HD), low(NX, NY, count, HD), low(NY, ends, count, HD),
            low(3, NY, count, HD), low(2, NY, count, HD), low(2, count, HD),
        )

    others = (max(tensors - 1, 1),)
    scratch = [
        low(length, width), low(width, features), low(width, 2 * HD),
        low(features, width), low(length, width), low(NY, NX, NZ * rows, length), low(length, HD),
        low(length, HD), low(NY, NX, NH, length, HD), low(NY, NX, NH, length, HD),
        low(2, columns, HD), low(2, HD, columns), low(3 * NX, NH * length, columns),
        full(2, HD, columns), full(2, HD, columns), low(HD, columns), low(HD, columns),
        low(HD, columns), low(HD, columns), full(2, 8, columns), full(2, 8, columns),
        low(NY, NX, NH, length, HD), low(NY, NX, NH, length, HD), full(length, HD),
        full(length, HD), low(tensors, share, width), low(others[0], share, width),
        low(tensors, share, width), low(others[0], share, width),
        low(NX - 1, NY, NZ * rows, length), low(length, 2 * HD), low(NX - 1, length, 2 * HD),
        low(NY, NZ, rows, 2 * HD), low(NZ - 1, NY, rows, 2 * HD), low(rows, 2 * HD),
        low(rows, 2 * HD),
        fold_room(NH, length), dma((6,)),
        (dma((2,)), dma((2,)), dma((3,)), dma((3,)), dma((4, 4)), dma((4, 4)), dma((4, 4, NX)),
         dma((4, 4, NX)), dma((NY, NH, 2)), dma((NY, NH, 2)), dma((NY, NH)), dma((NY, NH))),
    ]

    def fold_sems(ends):
        return (
            dma((4, 4, NX)), dma((4, 4, NX)), dma((NY, ends)), dma((NY, ends)),
            dma((NY, ends, 2)), dma((NY, ends, 2)), dma((4, 4)), dma((4, 4)), dma((3,)), dma((3,)),
            dma((2,)), dma((2,)),
        )

    scratch += [fold_sems(NH), dma((6,)), dma((6,)), dma((NZ - 1,)), dma((NZ - 1,))]
    scratch += [dma((7,)), dma((7,))] + [dma(others)] * 6
    results = pl.pallas_call(
        block_kernel,
        out_shape=(
            jax.ShapeDtypeStruct((share, width), BF16),
            jax.ShapeDtypeStruct((share, width), BF16),
            jax.ShapeDtypeStruct((length, HD), BF16),
            jax.ShapeDtypeStruct((rows, HD), F32),
            jax.ShapeDtypeStruct((rows, HD), F32),
        ),
        in_specs=[hbm, vmem, hbm, hbm, hbm, hbm, hbm, vmem],
        out_specs=(vmem,) * 5,
        scratch_shapes=scratch,
        compiler_params=pltpu.CompilerParams(
            collective_id=1, has_side_effects=True, vmem_limit_bytes=56 * 2**20
        ),
        name="attention_block",
    )(
        hidden_in.reshape(length, width), value_first.reshape(length, HD), w_query, w_key, w_value,
        w_out, grad_out.reshape(share, width), tables,
    )
    attn_out, grad_in, grad_first, key_weight, value_weight = pl.pallas_call(
        store_kernel,
        out_shape=tuple(jax.ShapeDtypeStruct(part.shape, part.dtype) for part in results),
        in_specs=[vmem] * len(results),
        out_specs=(vmem,) * len(results),
        name="store_results",
    )(*results)
    return (
        attn_out.reshape(1, share, width),
        grad_in.reshape(1, share, width),
        grad_first.reshape(1, length, HD),
        key_weight,
        value_weight,
    )


def solution(mesh):
    return jax.shard_map(
        shards,
        mesh=mesh,
        in_specs=(
            P("context", None, None),
            P("context", None, "tensor"),
            P(None, "tensor"),
            P(None, "tensor"),
            P(None, "tensor"),
            P("tensor", None),
            P(None, "tensor"),
            P("context", "tensor", None),
        ),
        out_specs=(
            P("context", "tensor", None),
            P("context", "tensor", None),
            P("context", None, "tensor"),
            P("context", "tensor"),
            P("context", "tensor"),
        ),
        check_vma=False,
    )
```
